32 devices in a mesh: tm: 4 (over y, x), space: 8 (over z, core).
Axes of the slice: x: 2, y: 2, z: 4, core: 2. Of those that a mesh axis runs over, the one named last changes fastest.
Arguments:
- features: float32 [12, 32, 16, 16, 64], P(None, None, 'tm', 'space'), may hold values from -6 to 6
- conv_first: float32 [32, 32, 3, 3, 3], replicated, may hold values from -0.21875 to 0.21875
- gain_first: float32 [32], replicated, may hold values from 0.25 to 1.75
- shift_first: float32 [32], replicated, may hold values from -3 to 3
- conv_second: float32 [32, 32, 3, 3, 3], replicated, may hold values from -0.21875 to 0.21875
- gain_second: float32 [32], replicated, may hold values from 0.25 to 1.75
- shift_second: float32 [32], replicated, may hold values from -3 to 3
- weight_one: float32 [512, 35], replicated, may hold values from -1 to 1
- bias_one: float32 [512], replicated, may hold values from -3 to 3
- weight_two: float32 [512, 512], replicated, may hold values from -0.25 to 0.25
- bias_two: float32 [512], replicated, may hold values from -3 to 3
- weight_three: float32 [512, 512], replicated, may hold values from -0.25 to 0.25
- bias_three: float32 [512], replicated, may hold values from -3 to 3
- weight_four: float32 [4, 512], replicated, may hold values from -0.25 to 0.25
- bias_four: float32 [4], replicated, may hold values from -3 to 3
- query_cells: int32 [3, 12, 32768], P(None, None, ('tm', 'space')), may hold values from 0 to 62, as said below
- field_cotangent: float32 [4, 12, 32768], P(None, None, ('tm', 'space')), may hold values from -6 to 6
- pooled_cotangent: float32 [12, 32, 8, 8, 32], P(None, None, 'tm', 'space'), may hold values from -6 to 6
Outputs:
- fields: float32 [4, 12, 32768], P(None, None, ('tm', 'space'))
- pooled: float32 [12, 32, 8, 8, 32], P(None, None, 'tm', 'space')
- grad_features: float32 [12, 32, 16, 16, 64], P(None, None, 'tm', 'space')
- grad_conv_first: float32 [32, 32, 3, 3, 3], replicated
- grad_gain_first: float32 [32], replicated
- grad_shift_first: float32 [32], replicated
- grad_conv_second: float32 [32, 32, 3, 3, 3], replicated
- grad_gain_second: float32 [32], replicated
- grad_shift_second: float32 [32], replicated
- grad_weight_one: float32 [512, 35], replicated
- grad_bias_one: float32 [512], replicated
- grad_weight_two: float32 [512, 512], replicated
- grad_bias_two: float32 [512], replicated
- grad_weight_three: float32 [512, 512], replicated
- grad_bias_three: float32 [512], replicated
- grad_weight_four: float32 [4, 512], replicated
- grad_bias_four: float32 [4], replicated
The draws below stay inside these ranges and needn't reach their ends.
Inputs may be any that keep to these rules, and one draw needn't show every extreme that they name: `query_cells`: component 0 is a time cell, 1 a height cell, 2 a width cell; the queries at positions s * 1024 to (s + 1) * 1024 - 1 of the last dimension lie in time cells (s // 8) * 4 to (s // 8 + 1) * 4 - 1 and height cells (s % 8) * 2 to (s % 8 + 1) * 2 - 1; width cells go from 0 to 62.
All inputs are finite; a program needn't handle non-finite values.
Results may differ from the reference program's by a relative error of at most 0.0003.
Values sent between devices are 32-bit elements; how exact they have to be, the bound alone decides.
A program may use at most 320 MiB of HBM per device.

```python
import jax
import jax.numpy as jnp
from jax import lax

CHANNELS = 32
HIDDEN_SIZE = 512
FIELDS = 4
CROPS = 12
SLAB = 4
ROWS = 2
WIDTH = 64
QUERY_DEV = 1024
DEPTH = 16
HEIGHT = 16
QUERIES = 32768
N_SPACE = 8


def draw_query_cells(key, part):
    key = jax.random.fold_in(key, 11)
    key_time, key_rows, key_width = jax.random.split(key, 3)
    position = jnp.arange(QUERIES, dtype=jnp.int32)
    block = position // QUERY_DEV
    within = position % QUERY_DEV
    slab_index = block // N_SPACE
    rows_index = block % N_SPACE
    time_cell = slab_index[None, :] * SLAB + jax.random.randint(key_time, (CROPS, QUERIES), 0, SLAB)
    rows_cell = rows_index[None, :] * ROWS + jax.random.randint(key_rows, (CROPS, QUERIES), 0, ROWS)
    width_cell = jax.random.randint(key_width, (CROPS, QUERIES), 0, WIDTH - 1)
    upper = (within == 0)[None, :]
    lower = (within == 1)[None, :]
    time_cell = jnp.where(upper, slab_index[None, :] * SLAB + SLAB - 1, jnp.where(lower, slab_index[None, :] * SLAB, time_cell))
    rows_cell = jnp.where(upper, rows_index[None, :] * ROWS + ROWS - 1, jnp.where(lower, rows_index[None, :] * ROWS, rows_cell))
    width_cell = jnp.where(upper, WIDTH - 2, jnp.where(lower, 0, width_cell))
    return jnp.stack([time_cell, rows_cell, width_cell], axis=0).astype(jnp.int32)


def levels(stream_key, dims, cuts, low, top_value):
    level = 1.0
    for dim, parts in cuts:
        heights = jax.random.uniform(jax.random.fold_in(jax.random.fold_in(stream_key, 6), dim), (parts,), jnp.float32, low / len(cuts), top_value / len(cuts))
        level = level * jnp.repeat(jnp.exp(heights), dims[dim] // parts).reshape((-1,) + (1,) * (len(dims) - 1 - dim))
    return level


def scatter_about(own_key, dims, scale, bound, cuts=(), kind=jnp.bfloat16):
    level = levels(own_key, dims, cuts, -0.22, 0.18) if cuts else 1.0
    result = jax.random.normal(own_key, dims, jnp.float32) * scale * level
    return jnp.minimum(jnp.maximum(result, -bound), bound).astype(kind)


def setup_inputs(seed: int = 0) -> dict:
    streams_of = jax.random.split(jax.random.key(seed), 19)
    features = scatter_about(streams_of[0], (CROPS, CHANNELS, DEPTH, HEIGHT, WIDTH), 1.0, 6.0, ((2, 4), (3, 8)), jnp.float32)
    conv_first = scatter_about(streams_of[1], (CHANNELS, CHANNELS, 3, 3, 3), (27 * CHANNELS) ** -0.5, 0.21875, (), jnp.float32)
    gain_first = jnp.clip(1.0 + 0.15 * jax.random.normal(streams_of[2], (CHANNELS,), jnp.float32), 0.25, 1.75)
    shift_first = scatter_about(streams_of[3], (CHANNELS,), 0.5, 3.0, (), jnp.float32)
    conv_second = scatter_about(streams_of[4], (CHANNELS, CHANNELS, 3, 3, 3), (27 * CHANNELS) ** -0.5, 0.21875, (), jnp.float32)
    gain_second = jnp.clip(1.0 + 0.15 * jax.random.normal(streams_of[5], (CHANNELS,), jnp.float32), 0.25, 1.75)
    shift_second = scatter_about(streams_of[6], (CHANNELS,), 0.5, 3.0, (), jnp.float32)
    weight_one = scatter_about(streams_of[7], (HIDDEN_SIZE, CHANNELS + 3), (CHANNELS + 3) ** -0.5, 1.0, (), jnp.float32)
    bias_one = scatter_about(streams_of[8], (HIDDEN_SIZE,), 0.5, 3.0, (), jnp.float32)
    weight_two = scatter_about(streams_of[9], (HIDDEN_SIZE, HIDDEN_SIZE), HIDDEN_SIZE ** -0.5, 0.25, (), jnp.float32)
    bias_two = scatter_about(streams_of[10], (HIDDEN_SIZE,), 0.5, 3.0, (), jnp.float32)
    weight_three = scatter_about(streams_of[11], (HIDDEN_SIZE, HIDDEN_SIZE), HIDDEN_SIZE ** -0.5, 0.25, (), jnp.float32)
    bias_three = scatter_about(streams_of[12], (HIDDEN_SIZE,), 0.5, 3.0, (), jnp.float32)
    weight_four = scatter_about(streams_of[13], (FIELDS, HIDDEN_SIZE), HIDDEN_SIZE ** -0.5, 0.25, (), jnp.float32)
    bias_four = scatter_about(streams_of[14], (FIELDS,), 0.5, 3.0, (), jnp.float32)
    query_cells = draw_query_cells(jax.random.fold_in(streams_of[18], 71), 0)
    field_cotangent = scatter_about(streams_of[16], (FIELDS, CROPS, QUERIES), 1.0, 6.0, ((2, 32),), jnp.float32)
    pooled_cotangent = scatter_about(streams_of[17], (CROPS, CHANNELS, DEPTH // 2, HEIGHT // 2, WIDTH // 2), 1.0, 6.0, ((2, 4), (3, 8)), jnp.float32)
    return {"features": features, "conv_first": conv_first, "gain_first": gain_first, "shift_first": shift_first, "conv_second": conv_second, "gain_second": gain_second, "shift_second": shift_second, "weight_one": weight_one, "bias_one": bias_one, "weight_two": weight_two, "bias_two": bias_two, "weight_three": weight_three, "bias_three": bias_three, "weight_four": weight_four, "bias_four": bias_four, "query_cells": query_cells, "field_cotangent": field_cotangent, "pooled_cotangent": pooled_cotangent}


eps = 1e-05
fraction_time = 0.25
fraction_rows = 0.5
fraction_width = 0.75

def convolve(padded, kernel, depth, height, width):
    total = jnp.zeros((padded.shape[0], kernel.shape[0], depth, height, width), jnp.float32)
    for a in range(3):
        for b in range(3):
            for e in range(3):
                window = padded[:, :, a:a + depth, b:b + height, e:e + width]
                total = total + jnp.einsum('oc,ncthw->nothw', kernel[:, :, a, b, e], window, precision=lax.Precision.HIGHEST)
    return total

def pad_grid(grid):
    return jnp.pad(grid, ((0, 0), (0, 0), (1, 1), (1, 1), (1, 1)))

def spread(vector):
    return vector[None, :, None, None, None]

def batch_norm(values, gain, shift):
    mean = lax.optimization_barrier(jnp.mean(values, axis=(0, 2, 3, 4)))
    centered = values - spread(mean)
    variance = lax.optimization_barrier(jnp.mean(centered * centered, axis=(0, 2, 3, 4)))
    return spread(gain) * centered * spread(lax.rsqrt(variance + eps)) + spread(shift)

def sample(padded, time_low, rows_low, width_low):
    crops, chans, span_time, span_rows, span_width = padded.shape
    flat = padded.reshape(crops, chans, span_time * span_rows * span_width)
    total = jnp.zeros((crops, chans, time_low.shape[1]), jnp.float32)
    for dt in range(2):
        for dh in range(2):
            for dw in range(2):
                factor = (fraction_time if dt else 1.0 - fraction_time) * (fraction_rows if dh else 1.0 - fraction_rows) * (fraction_width if dw else 1.0 - fraction_width)
                index = ((time_low + dt) * span_rows + rows_low + dh) * span_width + width_low + dw
                total = total + factor * jnp.take_along_axis(flat, index[:, None, :].astype(jnp.int32), axis=2)
    return total

def query_net(params, inputs):
    weight_one, bias_one, weight_two, bias_two, weight_three, bias_three, weight_four, bias_four = params
    high = lax.Precision.HIGHEST
    layer = jax.nn.softplus(jnp.dot(weight_one, inputs, precision=high) + bias_one[:, None])
    layer = jax.nn.softplus(jnp.dot(weight_two, layer, precision=high) + bias_two[:, None])
    layer = jax.nn.softplus(jnp.dot(weight_three, layer, precision=high) + bias_three[:, None])
    return jnp.dot(weight_four, layer, precision=high) + bias_four[:, None]

def forward(features, conv_first, gain_first, shift_first, conv_second, gain_second, shift_second, weight_one, bias_one, weight_two, bias_two, weight_three, bias_three, weight_four, bias_four, query_cells):
    crops, chans, depth, height, width = features.shape
    first = convolve(pad_grid(features), conv_first, depth, height, width)
    hidden = jax.nn.softplus(batch_norm(first, gain_first, shift_first))
    second = convolve(pad_grid(hidden), conv_second, depth, height, width)
    summed = batch_norm(second, gain_second, shift_second) + features
    latent = jax.nn.softplus(summed)
    pooled = latent.reshape(crops, chans, depth // 2, 2, height // 2, 2, width // 2, 2).mean(axis=(3, 5, 7))
    sampled = sample(pad_grid(latent), query_cells[0] + 1, query_cells[1] + 1, query_cells[2] + 1)
    coords = jnp.stack([2.0 * (query_cells[0].astype(jnp.float32) + fraction_time) / depth - 1.0, 2.0 * (query_cells[1].astype(jnp.float32) + fraction_rows) / height - 1.0, 2.0 * (query_cells[2].astype(jnp.float32) + fraction_width) / width - 1.0], axis=1)
    inputs = jnp.concatenate([sampled, coords], axis=1)
    params = (weight_one, bias_one, weight_two, bias_two, weight_three, bias_three, weight_four, bias_four)
    per_crop = jax.checkpoint(lambda block: query_net(params, block))
    fields = lax.map(per_crop, inputs)
    return (jnp.transpose(fields, (1, 0, 2)), pooled)

def reference(features, conv_first, gain_first, shift_first, conv_second, gain_second, shift_second, weight_one, bias_one, weight_two, bias_two, weight_three, bias_three, weight_four, bias_four, query_cells, field_cotangent, pooled_cotangent):

    def wrapped(*floats):
        return forward(*floats, query_cells)
    outputs, back = jax.vjp(wrapped, features, conv_first, gain_first, shift_first, conv_second, gain_second, shift_second, weight_one, bias_one, weight_two, bias_two, weight_three, bias_three, weight_four, bias_four)
    grads = back((field_cotangent, pooled_cotangent))
    return (outputs[0], outputs[1], grads[0], grads[1], grads[2], grads[3], grads[4], grads[5], grads[6], grads[7], grads[8], grads[9], grads[10], grads[11], grads[12], grads[13], grads[14])
```

```python
import functools

import jax
import jax.numpy as jnp
from jax import lax
from jax.experimental import pallas as pl
from jax.experimental.pallas import tpu as pltpu
from jax.sharding import PartitionSpec as P

MESH = pl.DeviceIdType.MESH
VMEM = pltpu.VMEM
f32 = jnp.float32
bf16 = jnp.bfloat16

eps = 1e-05
fraction_time = 0.25
fraction_rows = 0.5
fraction_width = 0.75
chunk = 256
lanes = 128


def dot(a, b):
    return lax.dot_general(a, b, (((1,), (0,)), ((), ())), preferred_element_type=f32)


def dot_nt(a, b):
    return lax.dot_general(a, b, (((1,), (1,)), ((), ())), preferred_element_type=f32)


def halves(value):
    high = value.astype(bf16)
    return high, (value - high.astype(f32)).astype(bf16)


def softplus_parts(value):
    result = jnp.maximum(value, 0.0) + jnp.log(1.0 + jnp.exp(-jnp.abs(value)))
    return result, jnp.exp(value - result)


class Place:
    def __init__(self, sizes):
        self.size_tm = sizes["tm"]
        self.size_space = sizes["space"]
        self.devices = self.size_tm * self.size_space
        self.tm = lax.axis_index("tm")
        self.space = lax.axis_index("space")
        self.index = self.tm * self.size_space + self.space

    def along_tm(self, distance):
        return (lax.rem(self.tm + distance, self.size_tm), self.space)

    def along_space(self, distance):
        return (self.tm, lax.rem(self.space + distance, self.size_space))

    def other(self, distance):
        index = lax.rem(self.index + distance, self.devices)
        return (lax.div(index, self.size_space), lax.rem(index, self.size_space))

    def barrier(self):
        semaphore = pltpu.get_barrier_semaphore()
        for distance in range(1, self.devices):
            pl.semaphore_signal(
                semaphore, inc=1, device_id=self.other(distance), device_id_type=MESH
            )
        pl.semaphore_wait(semaphore, self.devices - 1)


def remote(source, target, send, receive, device):
    return pltpu.make_async_remote_copy(
        src_ref=source,
        dst_ref=target,
        send_sem=send,
        recv_sem=receive,
        device_id=device,
        device_id_type=MESH,
    )


class Halo:
    def __init__(self, place, grid, send, receive):
        span, wide = grid.shape[0], grid.shape[1]
        top, side = span - 1, wide - 1
        inner_t, inner_h = pl.ds(1, span - 2), pl.ds(1, wide - 2)
        up_t, down_t = place.along_tm(1), place.along_tm(place.size_tm - 1)
        up_h, down_h = place.along_space(1), place.along_space(place.size_space - 1)
        low_t, high_t = place.tm > 0, place.tm < place.size_tm - 1
        low_h, high_h = place.space > 0, place.space < place.size_space - 1

        def one(index):
            return pl.ds(index, 1)

        both = jnp.logical_and
        table = [
            (high_t, low_t, (one(top - 1), inner_h), (one(0), inner_h), up_t),
            (low_t, high_t, (one(1), inner_h), (one(top), inner_h), down_t),
            (high_h, low_h, (inner_t, one(side - 1)), (inner_t, one(0)), up_h),
            (low_h, high_h, (inner_t, one(1)), (inner_t, one(side)), down_h),
            (both(high_h, low_t), both(low_h, low_t), (one(0), one(side - 1)), (one(0), one(0)), up_h),
            (both(low_h, low_t), both(high_h, low_t), (one(0), one(1)), (one(0), one(side)), down_h),
            (both(high_h, high_t), both(low_h, high_t), (one(top), one(side - 1)), (one(top), one(0)), up_h),
            (both(low_h, high_t), both(high_h, high_t), (one(top), one(1)), (one(top), one(side)), down_h),
        ]
        self.sends = [entry[0] for entry in table]
        self.receives = [entry[1] for entry in table]
        self.copies = [
            remote(grid.at[entry[2]], grid.at[entry[3]], send.at[i], receive.at[i], entry[4])
            for i, entry in enumerate(table)
        ]
        self.grid = grid
        self.edges = (low_t, high_t, low_h, high_h)

    def clear(self):
        grid = self.grid
        span, wide = grid.shape[0], grid.shape[1]
        layer, column = (1,) + grid.shape[1:], (span, 1) + grid.shape[2:]
        low_t, high_t, low_h, high_h = [jnp.logical_not(edge) for edge in self.edges]

        @pl.when(low_t)
        def _():
            grid[0:1] = jnp.zeros(layer, f32)

        @pl.when(high_t)
        def _():
            grid[span - 1 : span] = jnp.zeros(layer, f32)

        @pl.when(low_h)
        def _():
            grid[:, 0:1] = jnp.zeros(column, f32)

        @pl.when(high_h)
        def _():
            grid[:, wide - 1 : wide] = jnp.zeros(column, f32)

    def inside(self, t, h):
        span, wide = self.grid.shape[0], self.grid.shape[1]
        low_t, high_t, low_h, high_h = self.edges
        conditions = []
        if t == 0:
            conditions.append(low_t)
        if t == span - 1:
            conditions.append(high_t)
        if h == 0:
            conditions.append(low_h)
        if h == wide - 1:
            conditions.append(high_h)
        if not conditions:
            return None
        result = conditions[0].astype(f32)
        for condition in conditions[1:]:
            result = result * condition.astype(f32)
        return result

    def inner(self):
        span, wide = self.grid.shape[0], self.grid.shape[1]
        return [(t, h) for t in range(1, span - 1) for h in range(1, wide - 1)]

    def rim(self):
        span, wide = self.grid.shape[0], self.grid.shape[1]
        inner = self.inner()
        return [(t, h) for t in range(span) for h in range(wide) if (t, h) not in inner]

    def start(self, which):
        for i in which:

            @pl.when(self.sends[i])
            def _(i=i):
                self.copies[i].start()

    def arrive(self, which):
        for i in which:

            @pl.when(self.receives[i])
            def _(i=i):
                self.copies[i].wait_recv()

    def begin(self):
        self.start((1, 3, 0, 2))

    def pass_on(self):
        self.arrive((1,))
        self.start((7, 6))
        self.arrive((0,))
        self.start((5, 4))

    def finish(self):
        self.arrive((2, 3, 4, 5, 6, 7))
        for i in range(8):

            @pl.when(self.sends[i])
            def _(i=i):
                self.copies[i].wait_send()


class Share:
    def __init__(self, place, slots, send, receive):
        self.place = place
        self.slots = slots
        mine = slots.at[pl.ds(place.index, 1)]
        self.copies = [
            remote(mine, mine, send.at[d - 1], receive.at[d - 1], place.other(d))
            for d in range(1, place.devices)
        ]

    def start(self, value):
        self.slots[pl.ds(self.place.index, 1)] = value[None]
        for copy in self.copies:
            copy.start()

    def finish(self):
        for copy in self.copies:
            copy.wait_recv()
        for copy in self.copies:
            copy.wait_send()
        return self.slots[...]


class Reduction:
    def __init__(self, place, values, landing, inbox, whole, base, rows, order, send, receive):
        self.values, self.landing, self.inbox, self.whole = values, landing, inbox, whole
        self.base, self.rows = base, rows
        self.send, self.receive = send, receive
        self.stage = 0
        self.pending = None
        self.partners = []
        for axis, bit in order:
            mine = place.tm if axis == "tm" else place.space
            digit = lax.rem(lax.div(mine, bit), 2)
            partner = mine + bit * (1 - 2 * digit)
            device = (partner, place.space) if axis == "tm" else (place.tm, partner)
            self.partners.append((digit, device))
        half = values.shape[1] // 2
        digit, _ = self.partners[0]
        self.columns = pl.ds(pl.multiple_of(digit * half, lanes), half)
        self.others = pl.ds(pl.multiple_of((1 - digit) * half, lanes), half)
        self.kept = (base, rows)
        self.regions = []
        self.slot = pl.ds(base, rows)
        self.free = base

    def span(self, region):
        start, size = region
        return pl.ds(pl.multiple_of(start, 8), size)

    def move(self, source, target, device):
        self.pending = remote(
            source, target, self.send.at[self.stage], self.receive.at[self.stage], device
        )
        self.pending.start()

    def take(self, size):
        self.slot = pl.ds(self.free, size)
        self.free += size
        return self.inbox.at[self.slot]

    def step(self):
        last = len(self.partners) - 1
        stage = self.stage
        if self.pending is not None:
            self.pending.wait()
            self.pending = None
        if stage == 0:
            rows = self.span(self.kept)
            self.move(self.values.at[rows, self.others], self.landing.at[rows], self.partners[0][1])
        elif stage <= last:
            rows = self.span(self.kept)
            source = self.landing if stage == 1 else self.inbox
            self.values[rows, self.columns] += source[self.slot]
            digit, device = self.partners[stage]
            start, size = self.kept
            if stage < last:
                half = size // 2
                self.regions.append(self.kept)
                self.kept = (start + digit * half, half)
                rows = self.span((start + (1 - digit) * half, half))
                size = half
            self.move(self.values.at[rows, self.columns], self.take(size), device)
        elif stage <= 2 * last:
            rows = self.span(self.kept)
            if stage == last + 1:
                self.whole[rows, self.columns] = self.values[rows, self.columns] + self.inbox[self.slot]
            region = self.whole.at[rows, self.columns]
            self.move(region, region, self.partners[2 * last - stage][1])
            if self.regions:
                self.kept = self.regions.pop()
        self.stage += 1


class KernelSum:
    def __init__(self, place, partial, pieces, rows_tm, whole, send, receive):
        self.place = place
        self.partial, self.pieces, self.rows_tm, self.whole = partial, pieces, rows_tm, whole
        n, m = place.size_space, place.size_tm
        size = pieces.shape[1]
        self.size = size
        mine = place.space

        def part(index):
            return partial.at[pl.ds(pl.multiple_of(index * size, 8), size)]

        self.own = part(mine)
        self.scatter = [
            remote(
                part(lax.rem(mine + d, n)),
                pieces.at[mine],
                send.at[d - 1],
                receive.at[d - 1],
                place.along_space(d),
            )
            for d in range(1, n)
        ]
        slot = rows_tm.at[place.tm]
        self.exchange = [
            remote(slot, slot, send.at[n - 2 + d], receive.at[n - 2 + d], place.along_tm(d))
            for d in range(1, m)
        ]
        slot = whole.at[mine]
        self.gather = [
            remote(slot, slot, send.at[n + m - 3 + d], receive.at[n + m - 3 + d], place.along_space(d))
            for d in range(1, n)
        ]

    def start(self, value):
        rows, total = value.shape[0], self.partial.shape[0]
        self.partial[0:rows] = value
        if total > rows:
            self.partial[rows:total] = jnp.zeros((total - rows, value.shape[1]), f32)
        for copy in self.scatter:
            copy.start()
        self.pieces[pl.ds(self.place.space, 1)] = self.own[...][None]

    def end(self, copies):
        for copy in copies:
            copy.wait_recv()
        for copy in copies:
            copy.wait_send()

    def across(self):
        self.end(self.scatter)
        total = added([self.pieces[i] for i in range(self.place.size_space)])
        self.rows_tm[pl.ds(self.place.tm, 1)] = total[None]
        for copy in self.exchange:
            copy.start()

    def back(self):
        self.end(self.exchange)
        total = added([self.rows_tm[i] for i in range(self.place.size_tm)])
        self.whole[pl.ds(self.place.space, 1)] = total[None]
        for copy in self.gather:
            copy.start()

    def finish(self):
        self.end(self.gather)


def added(parts):
    total = parts[0]
    for part in parts[1:]:
        total = total + part
    return total


def diagonal(shape):
    return lax.broadcasted_iota(jnp.int32, shape, 0) == lax.broadcasted_iota(jnp.int32, shape, 1)


def as_row(column, wide=lanes):
    shape = (column.shape[0], wide)
    return jnp.sum(jnp.where(diagonal(shape), jnp.broadcast_to(column, shape), 0.0), axis=0, keepdims=True)


def as_column(row, chans):
    shape = (chans, row.shape[1])
    return jnp.sum(jnp.where(diagonal(shape), jnp.broadcast_to(row, shape), 0.0), axis=1, keepdims=True)


def per_channel(values):
    return jnp.sum(added(values), axis=1, keepdims=True)


def local_moments(values):
    count = len(values) * values[0].shape[1]
    mean = per_channel(values) / count
    centered = [value - mean for value in values]
    squares = per_channel([value * value for value in centered])
    return jnp.concatenate([as_row(mean), as_row(squares)], axis=0)


def whole_moments(parts, count, chans):
    devices = parts.shape[0]
    means, squares = parts[:, 0:1], parts[:, 1:2]
    middle = jnp.sum(means, axis=0, keepdims=True) / devices
    offset = means - middle
    total = jnp.sum(squares + offset * offset * float(count), axis=0) / float(count * devices)
    return as_column(middle[0], chans), lax.rsqrt(as_column(total, chans) + eps)


def load_taps(kernel, taps, backward):
    chans = kernel.shape[3]
    taps[...] = jnp.zeros(taps.shape, f32)
    for a in range(3):
        for b in range(3):
            for e in range(3):
                tap = kernel[2 - a, 2 - b, 2 - e].T if backward else kernel[a, b, e]
                taps[(e * 3 + a) * 3 + b, :, 0:chans] = tap


def toeplitz(taps, high, low, rows):
    chans = taps.shape[1]
    high[...] = jnp.zeros(high.shape, bf16)
    low[...] = jnp.zeros(low.shape, bf16)
    size = rows * chans
    for e in range(3):
        for a in range(3):
            block = []
            for h in range(rows):
                parts = []
                for b in range(3):
                    tap = taps[(e * 3 + a) * 3 + b]
                    parts.append(pltpu.roll(tap, (h + b) * chans, 1) if h + b else tap)
                block.append(added(parts))
            top, bottom = halves(jnp.concatenate(block, axis=0))
            for t in range(2):
                place = (pl.ds((e * 2 + t) * size, size), pl.ds((t + a) * lanes, lanes))
                high[place] = top
                low[place] = bottom


def side_masks(shape, width):
    place = lax.rem(lax.broadcasted_iota(jnp.int32, shape, 1), width)
    return place > 0, place < width - 1


def later(value, inside):
    return jnp.where(inside, pltpu.roll(value, 1, 1), 0.0)


def earlier(value, inside):
    return jnp.where(inside, pltpu.roll(value, value.shape[1] - 1, 1), 0.0)


def convolve(high, low, grid_high, grid_low, rows, chans, width):
    depth = high.shape[1]
    size = 2 * rows * chans
    pairs = (grid_high.shape[0] - 2 * lanes) // (2 * lanes)
    result = []
    for pair in range(pairs):
        span = pl.ds(pair * 2 * lanes, depth)
        value = dot(high[...], grid_high[span])
        value = value + dot(high[...], grid_low[span])
        value = value + dot(low[...], grid_high[span])
        first, last = side_masks((size, value.shape[1]), width)
        result.append(
            later(value[0:size], first)
            + value[size : 2 * size]
            + earlier(value[2 * size : 3 * size], last)
        )
    flat = jnp.concatenate(result, axis=0)
    return [flat[i : i + chans] for i in range(0, flat.shape[0], chans)]


def kernel_gradient(grad, grid_high, grid_low, rows, width):
    chans = grad[0].shape[0]
    total = None
    for pair in range(len(grad) // (2 * rows)):
        block = jnp.concatenate(grad[2 * rows * pair : 2 * rows * (pair + 1)], axis=0)
        first, last = side_masks(block.shape, width)
        taps = jnp.concatenate([earlier(block, last), block, later(block, first)], axis=0)
        high, low = halves(taps)
        span = pl.ds(pair * 2 * lanes, 4 * lanes)
        value = dot_nt(high, grid_high[span])
        value = value + dot_nt(high, grid_low[span])
        value = value + dot_nt(low, grid_high[span])
        total = value if total is None else total + value
    half = rows * chans
    blocks = []
    for e in range(3):
        for a in range(3):
            block = added(
                [
                    total[(e * 2 + t) * half : (e * 2 + t + 1) * half, (t + a) * lanes : (t + a + 1) * lanes]
                    for t in range(2)
                ]
            )
            parts = [block[0:chans]]
            for h in range(1, rows):
                parts.append(pltpu.roll(block[h * chans : (h + 1) * chans], lanes - h * chans, 1))
            blocks.append(added(parts))
    return jnp.concatenate(blocks, axis=0)


class Loads:
    def __init__(self, pairs, semaphores):
        self.copies = [
            pltpu.make_async_copy(source, target, semaphores.at[i])
            for i, (source, target) in enumerate(pairs)
        ]

    def start(self, *which):
        for i in which:
            self.copies[i].start()

    def wait(self, *which):
        for i in which:
            self.copies[i].wait()


def forward_kernel(
    sizes,
    features,
    kernel_one,
    kernel_two,
    gain_one,
    shift_one,
    gain_two,
    shift_two,
    input_high_out,
    input_low_out,
    hidden_high_out,
    hidden_low_out,
    normed_one_out,
    normed_two_out,
    slope_one_out,
    slope_two_out,
    latent_out,
    pooled_out,
    scale_one,
    scale_two,
    grid_one,
    grid_two,
    grid_three,
    input_high,
    input_low,
    hidden_high,
    hidden_low,
    normed_one,
    normed_two,
    slope_one,
    slope_two,
    latent,
    pooled,
    taps,
    high,
    low,
    slots_one,
    slots_two,
    halo_send,
    halo_receive,
    share_send,
    share_receive,
    store_done,
):
    width, slab, rows, chans = sizes["width"], sizes["slab"], sizes["rows"], sizes["chans"]
    crops = features.shape[2]
    cells = crops * width
    count = slab * rows * cells
    wide = rows + 2
    place = Place(sizes)
    halos = [
        Halo(place, grid, halo_send.at[i], halo_receive.at[i])
        for i, grid in enumerate((grid_one, grid_two, grid_three))
    ]
    shares = [
        Share(place, slots, share_send.at[i], share_receive.at[i])
        for i, slots in enumerate((slots_one, slots_two))
    ]
    stores = Loads(
        [
            (input_high, input_high_out),
            (input_low, input_low_out),
            (hidden_high, hidden_high_out),
            (hidden_low, hidden_low_out),
            (normed_one, normed_one_out),
            (normed_two, normed_two_out),
            (slope_one, slope_one_out),
            (slope_two, slope_two_out),
            (latent, latent_out),
            (pooled, pooled_out),
        ],
        store_done,
    )
    inner, rim = halos[0].inner(), halos[0].rim()
    for halo in halos:
        halo.clear()
    for t in range(slab):
        for h in range(rows):
            for crop in range(crops):
                grid_one[t + 1, h + 1, :, crop * width : (crop + 1) * width] = features[t, h, crop]
    place.barrier()
    halos[0].begin()

    def keep(t, h, value, top, bottom):
        span = pl.ds((t * wide + h) * chans, chans)
        top[span], bottom[span] = halves(value)

    load_taps(kernel_one, taps.at[0], False)
    toeplitz(taps.at[0], high.at[0], low.at[0], rows)
    for t, h in inner:
        keep(t, h, grid_one[t, h], input_high, input_low)
    halos[0].pass_on()
    load_taps(kernel_two, taps.at[1], False)
    toeplitz(taps.at[1], high.at[1], low.at[1], rows)
    gains = [as_column(gain[...], chans) for gain in (gain_one, gain_two)]
    shifts = [as_column(shift[...], chans) for shift in (shift_one, shift_two)]
    halos[0].finish()
    for t, h in rim:
        keep(t, h, grid_one[t, h], input_high, input_low)
    stores.start(0, 1)

    values = convolve(high.at[0], low.at[0], input_high, input_low, rows, chans, width)
    shares[0].start(local_moments(values))
    for (t, h), value in zip(inner, values):
        grid_two[t, h] = value
    halos[1].begin()
    mean, scale = whole_moments(shares[0].finish(), count, chans)
    scale_one[...] = scale

    def first_layer(t, h):
        normed = (grid_two[t, h] - mean) * scale
        normed_one[t, h] = normed
        hidden, slope = softplus_parts(gains[0] * normed + shifts[0])
        inside = halos[1].inside(t, h)
        keep(t, h, hidden if inside is None else hidden * inside, hidden_high, hidden_low)
        return slope

    for t, h in inner:
        slope_one[t - 1, h - 1] = first_layer(t, h)
    halos[1].pass_on()
    stores.start(6)
    halos[1].finish()
    for t, h in rim:
        first_layer(t, h)
    stores.start(2, 3, 4)

    values = convolve(high.at[1], low.at[1], hidden_high, hidden_low, rows, chans, width)
    shares[1].start(local_moments(values))
    for (t, h), value in zip(inner, values):
        grid_three[t, h] = value
    halos[2].begin()
    mean, scale_again = whole_moments(shares[1].finish(), count, chans)
    scale_two[...] = scale_again

    def second_layer(t, h):
        normed = (grid_three[t, h] - mean) * scale_again
        normed_two[t, h] = normed
        return gains[1] * normed + shifts[1] + grid_one[t, h]

    for t, h in inner:
        value, slope = softplus_parts(second_layer(t, h))
        latent[t - 1, h - 1] = value
        slope_two[t - 1, h - 1] = slope
    halos[2].pass_on()
    stores.start(7)
    for t in range(slab // 2):
        pooled[t] = added([latent[2 * t + i, h] for i in range(2) for h in range(rows)])
    stores.start(9)
    halos[2].finish()
    for t, h in rim:
        value = second_layer(t, h)
        if t > 0 and h > 0:
            value, _ = softplus_parts(value)
            latent[t - 1, h - 1] = value * halos[2].inside(t, h)
    stores.start(5, 8)
    stores.wait(*range(10))


def query_kernel(
    sizes,
    latent,
    cells,
    cotangent,
    weight_one,
    bias_one,
    weight_two,
    bias_two,
    weight_three,
    bias_three,
    weight_four,
    bias_four,
    fields,
    grad_latent,
    grads,
    one,
    one_t,
    two,
    two_t,
    three,
    three_t,
    four,
    four_t,
    wide_two,
    wide_three,
    wide_four,
    pad_one,
    pad_four,
    along,
    plane,
    inputs,
    cot_pad,
    cot_sum,
    cots,
    grad_one,
    grad_four,
    grad_biases,
    h1,
    h2,
    h3,
    s1,
    s2,
    s3,
    g1,
    g2,
    g3,
):
    crop = pl.program_id(0)
    slab, rows, width, chans = sizes["slab"], sizes["rows"], sizes["width"], sizes["chans"]
    hidden = weight_two.shape[0]
    queries = cells.shape[2]
    span_time, span_rows = slab + 1, rows + 1
    size_one, size_four = pad_one.shape[0], pad_four.shape[0]

    @pl.when(crop == 0)
    def _():
        known = weight_one.shape[0]
        pad_one[...] = jnp.zeros(pad_one.shape, f32)
        pad_one[0:known] = weight_one[...]
        pad_one[known : known + 1] = bias_one[...]
        pad_four[...] = jnp.zeros(pad_four.shape, f32)
        pad_four[0 : weight_four.shape[0]] = weight_four[...]
        for source, target in ((pad_one, one), (pad_four, four_t)):
            top, bottom = [part.astype(f32) for part in halves(source[...])]
            rest = target.shape[1] - 4 * source.shape[0]
            stack = [top, top, bottom, bottom, jnp.zeros((rest, hidden), f32)]
            target[...] = jnp.concatenate(stack, axis=0).T.astype(bf16)
        for source, target in ((pad_one[0:chans], one_t), (pad_four[...], four), (weight_two[...], two), (weight_three[...], three)):
            top, bottom = halves(source)
            target[0 : source.shape[0]] = top
            target[source.shape[0] :] = bottom
        for source, target in ((weight_two, two_t), (weight_three, three_t)):
            top, bottom = halves(source[...].T)
            target[0:hidden] = top
            target[hidden:] = bottom
        for source, target in ((bias_two, wide_two), (bias_three, wide_three)):
            column = jnp.broadcast_to(source[...], (lanes, hidden)).T
            for start in range(0, chunk, lanes):
                target[:, start : start + lanes] = column
        kind = lax.broadcasted_iota(jnp.int32, wide_four.shape, 0)
        bias = jnp.zeros(wide_four.shape, f32)
        for i in range(weight_four.shape[0]):
            bias = jnp.where(kind == i, bias_four[i], bias)
        wide_four[...] = bias
        inputs[...] = jnp.zeros(inputs.shape, bf16)
        cots[...] = jnp.zeros(cots.shape, bf16)
        for target in (cot_pad, cot_sum, grad_one, grad_four, grad_biases, grads):
            target[...] = jnp.zeros(target.shape, f32)

    @pl.when(lax.rem(crop, 2) == 0)
    def _():
        grad_latent[...] = jnp.zeros(grad_latent.shape, f32)

    def product(weights, values, span):
        both = dot(weights[...], values[0:hidden, span])
        return both[0:hidden] + both[hidden:] + dot(weights[0:hidden], values[hidden:, span])

    def outer(grads, values):
        both = dot_nt(grads[...], values[0:hidden])
        return both[0:hidden] + both[hidden:] + dot_nt(grads[0:hidden], values[hidden:])

    def keep(target, span, value):
        top, bottom = halves(value)
        target[0:hidden, span] = top
        target[hidden:, span] = bottom

    spans = [slice(start, start + chunk) for start in range(0, queries, chunk)]
    latent_parts = jnp.concatenate(halves(latent[...]), axis=1)
    cot_pad[0 : cotangent.shape[1]] = cotangent[0]
    cot_sum[...] += cot_pad[...]
    offset_time = lax.axis_index("tm") * slab
    offset_rows = lax.axis_index("space") * rows
    offset_width = lax.rem(crop, 2) * width

    for span in spans:
        time = cells[0, pl.ds(crop, 1), span]
        row = cells[1, pl.ds(crop, 1), span]
        place = cells[2, pl.ds(crop, 1), span]
        lane = lax.broadcasted_iota(jnp.int32, (lanes, chunk), 0)
        low = place + offset_width
        weights = jnp.where(lane == low, 1.0 - fraction_width, jnp.where(lane == low + 1, fraction_width, 0.0))
        weights = weights.astype(bf16)
        along[0:lanes, span] = weights
        along[lanes:, span] = weights
        values = dot(latent_parts, along[:, span])
        sampled = None
        for t in range(span_time):
            local = time - offset_time
            weight_time = jnp.where(local == t, 1.0 - fraction_time, jnp.where(local == t - 1, fraction_time, 0.0))
            for h in range(span_rows):
                local = row - offset_rows
                weight_rows = jnp.where(local == h, 1.0 - fraction_rows, jnp.where(local == h - 1, fraction_rows, 0.0))
                weight = weight_time * weight_rows
                index = t * span_rows + h
                plane[index : index + 1, span] = weight
                part = weight * values[index * chans : (index + 1) * chans]
                sampled = part if sampled is None else sampled + part
        coords = [
            2.0 * (time.astype(f32) + fraction_time) / sizes["depth"] - 1.0,
            2.0 * (row.astype(f32) + fraction_rows) / sizes["height"] - 1.0,
            2.0 * (place.astype(f32) + fraction_width) / width - 1.0,
        ]
        kind = lax.broadcasted_iota(jnp.int32, (size_one - chans, chunk), 0)
        extra = jnp.where(kind == 3, 1.0, 0.0)
        for i, coord in enumerate(coords):
            extra = jnp.where(kind == i, coord, extra)
        top, bottom = halves(jnp.concatenate([sampled, extra], axis=0))
        size = top.shape[0]
        for i, part in enumerate((top, bottom, top, bottom)):
            inputs[i * size : (i + 1) * size, span] = part
        top, bottom = halves(cot_pad[:, span])
        size = top.shape[0]
        for i, part in enumerate((top, bottom, top, bottom)):
            cots[i * size : (i + 1) * size, span] = part

    for span in spans:
        value, slope = softplus_parts(dot(one[...], inputs[:, span]))
        keep(h1, span, value)
        s1[:, span] = slope
    for span in spans:
        value, slope = softplus_parts(product(two, h1, span) + wide_two[...])
        keep(h2, span, value)
        s2[:, span] = slope
    for span in spans:
        value, slope = softplus_parts(product(three, h2, span) + wide_three[...])
        keep(h3, span, value)
        s3[:, span] = slope
    for span in spans:
        grad = dot(four_t[...], cots[:, span]) * s3[:, span]
        keep(g3, span, grad)
        grad_biases[1] += added([grad[:, i : i + lanes] for i in range(0, chunk, lanes)])
    for span in spans:
        both = dot(four[...], h3[0:hidden, span])
        value = both[0:size_four] + both[size_four:] + dot(four[0:size_four], h3[hidden:, span])
        fields[0, :, span] = (value + wide_four[...])[0 : fields.shape[1]]
    grad_four[...] += dot_nt(h3[0:hidden], cots[...]) + dot_nt(h3[hidden:], cots[...])
    grads[hidden : 2 * hidden] += outer(g3, h2)
    for span in spans:
        grad = product(three_t, g3, span) * s2[:, span]
        keep(g2, span, grad)
        grad_biases[0] += added([grad[:, i : i + lanes] for i in range(0, chunk, lanes)])
    grads[0:hidden] += outer(g2, h1)
    for span in spans:
        keep(g1, span, product(two_t, g2, span) * s1[:, span])
    grad_one[...] += dot_nt(g1[0:hidden], inputs[0:lanes]) + dot_nt(g1[hidden:], inputs[0:lanes])
    for span in spans:
        both = dot(one_t[...], g1[0:hidden, span])
        grad = both[0:chans] + both[chans:] + dot(one_t[0:chans], g1[hidden:, span])
        spread = [plane[i : i + 1, span] * grad for i in range(span_time * span_rows)]
        top, bottom = halves(jnp.concatenate(spread, axis=0))
        grad_latent[...] += dot_nt(top, along[0:lanes, span]) + dot_nt(bottom, along[0:lanes, span])

    @pl.when(crop == pl.num_programs(0) - 1)
    def _():
        start = 2 * hidden
        for source, size in ((grad_one, size_one), (grad_four, size_four)):
            flat = source[...].T
            grads[start : start + size] = flat[0:size] + flat[size : 2 * size]
            start += size
        for i in range(2):
            grads[start + i : start + i + 1] = jnp.sum(grad_biases[i].T, axis=0, keepdims=True)
        total = jnp.sum(cot_sum[...], axis=1, keepdims=True)
        grads[start + 2 : start + 3] = as_row(total, hidden)


def backward_kernel(
    sizes,
    grad_latent_in,
    upsampled_in,
    input_high_in,
    input_low_in,
    hidden_high_in,
    hidden_low_in,
    normed_one_in,
    normed_two_in,
    slope_one_in,
    slope_two_in,
    grads_in,
    scale_one,
    scale_two,
    gain_one,
    gain_two,
    kernel_one,
    kernel_two,
    grad_features,
    grads_out,
    grad_kernels,
    sums,
    folded,
    upsampled,
    input_high,
    input_low,
    hidden_high,
    hidden_low,
    normed_one,
    normed_two,
    slope_one,
    slope_two,
    grads,
    landing,
    inbox,
    whole,
    arrived_time,
    arrived_rows,
    grid_one,
    grid_two,
    grid_high,
    grid_low,
    grad_summed,
    taps,
    high,
    low,
    partial,
    pieces,
    rows_tm,
    gathered,
    slots_one,
    slots_two,
    halo_send,
    halo_receive,
    share_send,
    share_receive,
    sum_send,
    sum_receive,
    reduce_send,
    reduce_receive,
    load_done,
):
    width, slab, rows, chans = sizes["width"], sizes["slab"], sizes["rows"], sizes["chans"]
    wide = rows + 2
    cells = upsampled.shape[2]
    crops = cells // width
    place = Place(sizes)
    count = float(slab * rows * cells * place.devices)
    halo_one = Halo(place, grid_one, halo_send.at[0], halo_receive.at[0])
    halo_two = Halo(place, grid_two, halo_send.at[1], halo_receive.at[1])
    share_one = Share(place, slots_one, share_send.at[0], share_receive.at[0])
    share_two = Share(place, slots_two, share_send.at[1], share_receive.at[1])
    kernel_sums = [
        KernelSum(
            place,
            partial.at[i],
            pieces.at[i],
            rows_tm.at[i],
            gathered.at[i],
            sum_send.at[i],
            sum_receive.at[i],
        )
        for i in range(2)
    ]
    bits_tm = [("tm", 1 << i) for i in range(place.size_tm.bit_length() - 1)]
    bits_space = [("space", 1 << i) for i in range(place.size_space.bit_length() - 1)]
    orders = [
        [bits_space[0]] + bits_tm[1:] + bits_space[1:] + bits_tm[:1],
        bits_space + bits_tm[1:] + bits_tm[:1],
    ]
    half = grads.shape[0] // 2
    reductions = [
        Reduction(
            place,
            grads,
            landing,
            inbox,
            whole,
            i * half,
            half,
            orders[i],
            reduce_send.at[i],
            reduce_receive.at[i],
        )
        for i in range(2)
    ]
    total_steps = 2 * len(orders[0])

    def reduce_step():
        for reduction in reductions:
            if reduction.stage < total_steps:
                reduction.step()

    loads = Loads(
        [
            (grad_latent_in, folded),
            (grads_in, grads),
            (upsampled_in, upsampled),
            (slope_two_in, slope_two),
            (normed_two_in, normed_two),
            (hidden_high_in, hidden_high),
            (hidden_low_in, hidden_low),
            (slope_one_in, slope_one),
            (normed_one_in, normed_one),
            (input_high_in, input_high),
            (input_low_in, input_low),
        ],
        load_done,
    )
    loads.start(*range(11))
    halo_one.clear()
    halo_two.clear()
    up_t, up_h = place.along_tm(1), place.along_space(1)
    low_t, high_t = place.tm > 0, place.tm < place.size_tm - 1
    low_h, high_h = place.space > 0, place.space < place.size_space - 1

    @pl.when(jnp.logical_not(low_t))
    def _():
        arrived_time[...] = jnp.zeros(arrived_time.shape, f32)

    @pl.when(jnp.logical_not(low_h))
    def _():
        arrived_rows[...] = jnp.zeros(arrived_rows.shape, f32)

    send, receive = halo_send.at[2], halo_receive.at[2]
    time_copy = remote(folded.at[pl.ds(slab, 1)], arrived_time, send.at[0], receive.at[0], up_t)
    rows_copy = remote(
        folded.at[pl.ds(1, slab - 1), pl.ds(rows, 1)],
        arrived_rows.at[pl.ds(1, slab - 1)],
        send.at[1],
        receive.at[1],
        up_h,
    )
    corner_copy = remote(
        folded.at[pl.ds(0, 1), pl.ds(rows, 1)],
        arrived_rows.at[pl.ds(0, 1)],
        send.at[2],
        receive.at[2],
        up_h,
    )
    loads.wait(0)
    place.barrier()

    @pl.when(high_t)
    def _():
        time_copy.start()

    @pl.when(high_h)
    def _():
        rows_copy.start()

    loads.wait(1)
    reduce_step()
    load_taps(kernel_two, taps.at[1], True)
    toeplitz(taps.at[1], high.at[1], low.at[1], rows)
    gains = [as_column(gain[...], chans) for gain in (gain_one, gain_two)]

    @pl.when(low_t)
    def _():
        time_copy.wait_recv()

    folded[0:1] += arrived_time[...]

    @pl.when(high_h)
    def _():
        corner_copy.start()

    reduce_step()
    load_taps(kernel_one, taps.at[0], True)
    toeplitz(taps.at[0], high.at[0], low.at[0], rows)

    @pl.when(low_h)
    def _():
        rows_copy.wait_recv()
        corner_copy.wait_recv()

    @pl.when(high_t)
    def _():
        time_copy.wait_send()

    @pl.when(high_h)
    def _():
        rows_copy.wait_send()
        corner_copy.wait_send()

    folded[0:slab, 0:1] += arrived_rows[...]
    loads.wait(2, 3, 4)

    inner, rim = halo_one.inner(), halo_one.rim()

    def norm_sums(grads_here, normed):
        cross = [grad * normed[t, h] for (t, h), grad in zip(inner, grads_here)]
        return jnp.concatenate(
            [as_row(per_channel(grads_here)), as_row(per_channel(cross))], axis=0
        )

    def norm_terms(parts, scale, gain):
        result = jnp.sum(parts, axis=0)
        total = as_column(result[0:1], chans) / count
        cross = as_column(result[1:2], chans) / count
        return result, total, cross, gain * scale[...]

    def keep(t, h, value):
        span = pl.ds((t * wide + h) * chans, chans)
        grid_high[span], grid_low[span] = halves(value)

    values = []
    for t, h in inner:
        value = folded[t - 1, h - 1] + upsampled[(t - 1) // 2]
        value = value * slope_two[t - 1, h - 1]
        grad_summed[t - 1, h - 1] = value
        grid_two[t, h] = value
        values.append(value)
    share_two.start(norm_sums(values, normed_two))
    halo_two.begin()
    result, total, cross, factor = norm_terms(share_two.finish(), scale_two, gains[1])
    sums[1] = result
    reduce_step()
    values = []
    for t, h in inner:
        value = factor * (grid_two[t, h] - total - normed_two[t, h] * cross)
        values.append(value)
        keep(t, h, value)
    halo_two.pass_on()
    loads.wait(5, 6)
    kernel_sums[1].start(kernel_gradient(values, hidden_high, hidden_low, rows, width))
    halo_two.finish()
    for t, h in rim:
        value = factor * (grid_two[t, h] - total - normed_two[t, h] * cross)
        keep(t, h, value * halo_two.inside(t, h))
    reduce_step()
    loads.wait(7, 8)
    values = convolve(high.at[1], low.at[1], grid_high, grid_low, rows, chans, width)
    values = [value * slope_one[t - 1, h - 1] for (t, h), value in zip(inner, values)]
    share_one.start(norm_sums(values, normed_one))
    for (t, h), value in zip(inner, values):
        grid_one[t, h] = value
    halo_one.begin()
    kernel_sums[1].across()
    reduce_step()
    result, total, cross, factor = norm_terms(share_one.finish(), scale_one, gains[0])
    sums[0] = result
    values = []
    for t, h in inner:
        value = factor * (grid_one[t, h] - total - normed_one[t, h] * cross)
        values.append(value)
        keep(t, h, value)
    halo_one.pass_on()
    kernel_sums[1].back()
    loads.wait(9, 10)
    kernel_sums[0].start(kernel_gradient(values, input_high, input_low, rows, width))
    reduce_step()
    halo_one.finish()
    for t, h in rim:
        value = factor * (grid_one[t, h] - total - normed_one[t, h] * cross)
        keep(t, h, value * halo_one.inside(t, h))
    reduce_step()
    values = convolve(high.at[0], low.at[0], grid_high, grid_low, rows, chans, width)
    kernel_sums[0].across()
    reduce_step()
    for (t, h), value in zip(inner, values):
        value = value + grad_summed[t - 1, h - 1]
        for crop in range(crops):
            grad_features[t - 1, h - 1, crop] = value[:, crop * width : (crop + 1) * width]
    kernel_sums[0].back()
    while reductions[0].stage < total_steps:
        reduce_step()
    grads_out[...] = whole[...]
    for i in range(2):
        kernel_sums[i].finish()
        size = grad_kernels.shape[1]
        grad_kernels[i] = gathered[i].reshape(-1, lanes)[0:size]


def closing_kernel(
    sizes,
    grads,
    grad_kernels,
    sums,
    kernel_one,
    gain_one,
    shift_one,
    kernel_two,
    gain_two,
    shift_two,
    one,
    bias_one,
    two,
    bias_two,
    three,
    bias_three,
    four,
    bias_four,
):
    chans = sizes["chans"]
    hidden = two.shape[0]
    for i, kernel in enumerate((kernel_one, kernel_two)):
        for e in range(3):
            for a in range(3):
                block = grad_kernels[i, (e * 3 + a) * chans : (e * 3 + a + 1) * chans]
                for b in range(3):
                    kernel[a, b, e] = block[:, b * chans : (b + 1) * chans]
    for i, (gain, shift) in enumerate(((gain_one, shift_one), (gain_two, shift_two))):
        shift[...] = sums[i, 0:1, 0:chans]
        gain[...] = sums[i, 1:2, 0:chans]
    two[...] = grads[0:hidden]
    three[...] = grads[hidden : 2 * hidden]
    start = 2 * hidden
    known = one.shape[0]
    one[...] = grads[start : start + known]
    bias_one[...] = grads[start + known : start + known + 1]
    start += sizes["rows_one"]
    four[...] = grads[start : start + four.shape[0]]
    start += sizes["rows_four"]
    bias_two[...] = grads[start : start + 1]
    bias_three[...] = grads[start + 1 : start + 2]
    bias_four[...] = grads[start + 2 : start + 3, 0 : bias_four.shape[1]]


def in_vmem(count):
    return [pl.BlockSpec(memory_space=VMEM)] * count


def anywhere(count):
    return [pl.BlockSpec(memory_space=pl.ANY)] * count


def struct(shape, dtype=f32):
    return jax.ShapeDtypeStruct(shape, dtype)


def scratch(structs):
    return [VMEM(item.shape, item.dtype) for item in structs]


def per_device(
    mesh_sizes,
    features,
    conv_first,
    gain_first,
    shift_first,
    conv_second,
    gain_second,
    shift_second,
    weight_one,
    bias_one,
    weight_two,
    bias_two,
    weight_three,
    bias_three,
    weight_four,
    bias_four,
    query_cells,
    field_cotangent,
    pooled_cotangent,
):
    crops, chans, slab, rows, width = features.shape
    queries = query_cells.shape[2]
    hidden, known = weight_one.shape
    field_count = weight_four.shape[0]
    size_tm, size_space = mesh_sizes
    devices = size_tm * size_space
    cells = crops * width
    rows_one = -(-(known + 1) // 16) * 16
    rows_four = 16
    sizes = {
        "tm": size_tm,
        "space": size_space,
        "slab": slab,
        "rows": rows,
        "width": width,
        "chans": chans,
        "depth": slab * size_tm,
        "height": rows * size_space,
        "rows_one": rows_one,
        "rows_four": rows_four,
    }
    span, wide = slab + 2, rows + 2
    matrix = (2, 6 * rows * chans, 4 * wide * chans)
    taps = VMEM((2, 27, chans, lanes), f32)
    memory = pltpu.CompilerParams(vmem_limit_bytes=56 * 2**20)

    grid = jnp.transpose(features, (2, 3, 0, 1, 4))
    kernels = [jnp.transpose(kernel, (2, 3, 4, 0, 1)) for kernel in (conv_first, conv_second)]
    gains = [gain_first[None], gain_second[None]]
    shifts = [shift_first[None], shift_second[None]]
    block = struct((slab, rows, chans, cells))
    padded = struct((span, wide, chans, cells))
    flat = struct((span * wide * chans, cells), bf16)
    column = struct((chans, 1))
    slots = VMEM((devices, 2, lanes), f32)
    kept = [flat] * 4 + [padded] * 2 + [block] * 2
    kept += [struct((slab + 1, rows + 1, chans, cells)), struct((slab // 2, chans, cells))]
    copies = pltpu.SemaphoreType.DMA
    (
        input_high,
        input_low,
        hidden_high,
        hidden_low,
        normed_one,
        normed_two,
        slope_one,
        slope_two,
        latent,
        pool_part,
        scale_one,
        scale_two,
    ) = pl.pallas_call(
        functools.partial(forward_kernel, sizes),
        out_shape=kept + [column] * 2,
        in_specs=in_vmem(7),
        out_specs=anywhere(10) + in_vmem(2),
        scratch_shapes=[
            *scratch([padded] * 3 + kept),
            taps,
            VMEM(matrix, bf16),
            VMEM(matrix, bf16),
            slots,
            slots,
            copies((3, 8)),
            copies((3, 8)),
            copies((2, devices - 1)),
            copies((2, devices - 1)),
            copies((10,)),
        ],
        compiler_params=pltpu.CompilerParams(
            collective_id=0, has_side_effects=True, vmem_limit_bytes=56 * 2**20
        ),
        name="forward_block",
    )(grid, *kernels, gains[0], shifts[0], gains[1], shifts[1])
    pooled = pool_part.reshape(slab // 2, chans, crops, width // 2, 2).sum(axis=4) * (0.25 / rows)
    pooled = jnp.transpose(pooled, (2, 1, 0, 3))[:, :, :, None, :]

    sample_rows = (slab + 1) * (rows + 1)
    unit = 8 << (devices.bit_length() - 3)
    reduce_rows = -(-(2 * hidden + rows_one + rows_four + 8) // (2 * unit)) * 2 * unit
    pair_block = pl.BlockSpec((sample_rows * chans, lanes), lambda n: (0, n // 2))
    crop_block = pl.BlockSpec((1, field_count, queries), lambda n: (n, 0, 0))

    def constant(shape):
        return pl.BlockSpec(shape, lambda n: (0,) * len(shape))

    operands = [
        latent.reshape(sample_rows * chans, cells),
        query_cells,
        jnp.transpose(field_cotangent, (1, 0, 2)),
        jnp.transpose(weight_one),
        bias_one[None],
        weight_two,
        bias_two[None],
        weight_three,
        bias_three[None],
        weight_four,
        bias_four,
    ]
    specs = [pair_block, constant(query_cells.shape), crop_block]
    specs += [constant(operand.shape) for operand in operands[3:-1]]
    specs += [pl.BlockSpec(memory_space=pltpu.SMEM)]
    outs = [
        struct((crops, field_count, queries)),
        struct((sample_rows * chans, cells)),
        struct((reduce_rows, hidden)),
    ]
    fields, grad_latent, grads = pl.pallas_call(
        functools.partial(query_kernel, sizes),
        grid=(crops,),
        out_shape=outs,
        in_specs=specs,
        out_specs=[crop_block, pair_block, constant(outs[2].shape)],
        scratch_shapes=[
            VMEM((hidden, 256), bf16),
            VMEM((2 * chans, hidden), bf16),
            *[VMEM((2 * hidden, hidden), bf16)] * 4,
            VMEM((2 * rows_four, hidden), bf16),
            VMEM((hidden, lanes), bf16),
            VMEM((hidden, chunk), f32),
            VMEM((hidden, chunk), f32),
            VMEM((rows_four, chunk), f32),
            VMEM((rows_one, hidden), f32),
            VMEM((rows_four, hidden), f32),
            VMEM((2 * lanes, queries), bf16),
            VMEM((-(-sample_rows // 8) * 8, queries), f32),
            VMEM((256, queries), bf16),
            VMEM((rows_four, queries), f32),
            VMEM((rows_four, queries), f32),
            VMEM((lanes, queries), bf16),
            VMEM((hidden, lanes), f32),
            VMEM((hidden, lanes), f32),
            VMEM((2, hidden, lanes), f32),
            *[VMEM((2 * hidden, queries), bf16)] * 3,
            *[VMEM((hidden, queries), f32)] * 3,
            *[VMEM((2 * hidden, queries), bf16)] * 3,
        ],
        compiler_params=pltpu.CompilerParams(
            dimension_semantics=("arbitrary",), vmem_limit_bytes=56 * 2**20
        ),
        name="query_network",
    )(*operands)

    upsampled = jnp.transpose(pooled_cotangent[:, :, :, 0], (2, 1, 0, 3)) * (0.25 / rows)
    upsampled = jnp.broadcast_to(upsampled[..., None], upsampled.shape + (2,))
    upsampled = upsampled.reshape(slab // 2, chans, cells)
    kernel_rows = 9 * chans
    piece = -(-kernel_rows // (8 * size_space)) * 8
    sum_copies = 2 * size_space + size_tm - 3
    reduce_block = struct((reduce_rows, hidden))
    half_block = struct((reduce_rows, hidden // 2))
    loaded = [struct((slab + 1, rows + 1, chans, cells)), struct((slab // 2, chans, cells))]
    loaded += [flat] * 4 + [padded] * 2 + [block] * 2 + [reduce_block]
    grad_features, grads, grad_kernels, sums = pl.pallas_call(
        functools.partial(backward_kernel, sizes),
        out_shape=[
            struct((slab, rows, crops, chans, width)),
            reduce_block,
            struct((2, kernel_rows, lanes)),
            struct((2, 2, lanes)),
        ],
        in_specs=anywhere(11) + in_vmem(6),
        out_specs=in_vmem(4),
        scratch_shapes=[
            *scratch(loaded),
            *scratch([half_block] * 2 + [reduce_block]),
            VMEM((1, rows + 1, chans, cells), f32),
            VMEM((slab, 1, chans, cells), f32),
            *scratch([padded] * 2 + [flat] * 2 + [block]),
            taps,
            VMEM(matrix, bf16),
            VMEM(matrix, bf16),
            VMEM((2, size_space * piece, lanes), f32),
            VMEM((2, size_space, piece, lanes), f32),
            VMEM((2, size_tm, piece, lanes), f32),
            VMEM((2, size_space, piece, lanes), f32),
            slots,
            slots,
            copies((3, 8)),
            copies((3, 8)),
            copies((2, devices - 1)),
            copies((2, devices - 1)),
            copies((2, sum_copies)),
            copies((2, sum_copies)),
            copies((2, 2 * devices.bit_length())),
            copies((2, 2 * devices.bit_length())),
            copies((11,)),
        ],
        compiler_params=pltpu.CompilerParams(
            collective_id=1, has_side_effects=True, vmem_limit_bytes=56 * 2**20
        ),
        name="backward_block",
    )(
        grad_latent.reshape(slab + 1, rows + 1, chans, cells),
        upsampled,
        input_high,
        input_low,
        hidden_high,
        hidden_low,
        normed_one,
        normed_two,
        slope_one,
        slope_two,
        grads,
        scale_one,
        scale_two,
        gains[0],
        gains[1],
        *kernels,
    )
    row = struct((1, chans))
    wide_row = struct((1, hidden))
    taps_shape = struct((3, 3, 3, chans, chans))
    closing = pl.pallas_call(
        functools.partial(closing_kernel, sizes),
        out_shape=[
            taps_shape,
            row,
            row,
            taps_shape,
            row,
            row,
            struct((known, hidden)),
            wide_row,
            struct((hidden, hidden)),
            wide_row,
            struct((hidden, hidden)),
            wide_row,
            struct((field_count, hidden)),
            struct((1, field_count)),
        ],
        in_specs=in_vmem(3),
        out_specs=in_vmem(14),
        compiler_params=memory,
        name="closing",
    )(grads, grad_kernels, sums)
    closing = list(closing)
    for i in (0, 3):
        closing[i] = jnp.transpose(closing[i], (3, 4, 0, 1, 2))
    closing[6] = jnp.transpose(closing[6])
    for i in (1, 2, 4, 5, 7, 9, 11, 13):
        closing[i] = closing[i][0]
    return (
        jnp.transpose(fields, (1, 0, 2)),
        pooled,
        jnp.transpose(grad_features, (2, 3, 0, 1, 4)),
        *closing,
    )


def solution(mesh):
    placed = (P(None, None, "tm", "space", None),) + (P(),) * 14
    placed += (P(None, None, ("tm", "space")),) * 2 + (P(None, None, "tm", "space", None),)
    return jax.shard_map(
        functools.partial(per_device, (mesh.shape["tm"], mesh.shape["space"])),
        mesh=mesh,
        in_specs=placed,
        out_specs=(
            P(None, None, ("tm", "space")),
            P(None, None, "tm", "space", None),
            P(None, None, "tm", "space", None),
        )
        + (P(),) * 14,
        check_vma=False,
    )
```

```python
import functools

import jax
import jax.numpy as jnp
from jax import lax
from jax.experimental import pallas as pl
from jax.experimental.pallas import tpu as pltpu
from jax.sharding import PartitionSpec as P

MESH = pl.DeviceIdType.MESH
VMEM = pltpu.VMEM
f32 = jnp.float32
bf16 = jnp.bfloat16

eps = 1e-05
fraction_time = 0.25
fraction_rows = 0.5
fraction_width = 0.75
chunk = 256
lanes = 128


def dot(a, b):
    return lax.dot_general(a, b, (((1,), (0,)), ((), ())), preferred_element_type=f32)


def dot_nt(a, b):
    return lax.dot_general(a, b, (((1,), (1,)), ((), ())), preferred_element_type=f32)


def halves(value):
    high = value.astype(bf16)
    return high, (value - high.astype(f32)).astype(bf16)


def softplus_parts(value):
    result = jnp.maximum(value, 0.0) + jnp.log(1.0 + jnp.exp(-jnp.abs(value)))
    return result, jnp.exp(value - result)


class Place:
    def __init__(self, sizes):
        self.size_tm = sizes["tm"]
        self.size_space = sizes["space"]
        self.devices = self.size_tm * self.size_space
        self.tm = lax.axis_index("tm")
        self.space = lax.axis_index("space")
        self.index = self.tm * self.size_space + self.space

    def along_tm(self, distance):
        return (lax.rem(self.tm + distance, self.size_tm), self.space)

    def along_space(self, distance):
        return (self.tm, lax.rem(self.space + distance, self.size_space))

    def other(self, distance):
        index = lax.rem(self.index + distance, self.devices)
        return (lax.div(index, self.size_space), lax.rem(index, self.size_space))

    def barrier(self):
        semaphore = pltpu.get_barrier_semaphore()
        for distance in range(1, self.devices):
            pl.semaphore_signal(
                semaphore, inc=1, device_id=self.other(distance), device_id_type=MESH
            )
        pl.semaphore_wait(semaphore, self.devices - 1)


def remote(source, target, send, receive, device):
    return pltpu.make_async_remote_copy(
        src_ref=source,
        dst_ref=target,
        send_sem=send,
        recv_sem=receive,
        device_id=device,
        device_id_type=MESH,
    )


class Halo:
    def __init__(self, place, grid, send, receive):
        span, wide = grid.shape[0], grid.shape[1]
        top, side = span - 1, wide - 1
        inner_t, inner_h = pl.ds(1, span - 2), pl.ds(1, wide - 2)
        up_t, down_t = place.along_tm(1), place.along_tm(place.size_tm - 1)
        up_h, down_h = place.along_space(1), place.along_space(place.size_space - 1)
        low_t, high_t = place.tm > 0, place.tm < place.size_tm - 1
        low_h, high_h = place.space > 0, place.space < place.size_space - 1

        def one(index):
            return pl.ds(index, 1)

        both = jnp.logical_and
        table = [
            (high_t, low_t, (one(top - 1), inner_h), (one(0), inner_h), up_t),
            (low_t, high_t, (one(1), inner_h), (one(top), inner_h), down_t),
            (high_h, low_h, (inner_t, one(side - 1)), (inner_t, one(0)), up_h),
            (low_h, high_h, (inner_t, one(1)), (inner_t, one(side)), down_h),
            (both(high_h, low_t), both(low_h, low_t), (one(0), one(side - 1)), (one(0), one(0)), up_h),
            (both(low_h, low_t), both(high_h, low_t), (one(0), one(1)), (one(0), one(side)), down_h),
            (both(high_h, high_t), both(low_h, high_t), (one(top), one(side - 1)), (one(top), one(0)), up_h),
            (both(low_h, high_t), both(high_h, high_t), (one(top), one(1)), (one(top), one(side)), down_h),
        ]
        self.sends = [entry[0] for entry in table]
        self.receives = [entry[1] for entry in table]
        self.copies = [
            remote(grid.at[entry[2]], grid.at[entry[3]], send.at[i], receive.at[i], entry[4])
            for i, entry in enumerate(table)
        ]
        self.grid = grid
        self.edges = (low_t, high_t, low_h, high_h)

    def clear(self):
        grid = self.grid
        span, wide = grid.shape[0], grid.shape[1]
        layer, column = (1,) + grid.shape[1:], (span, 1) + grid.shape[2:]
        low_t, high_t, low_h, high_h = [jnp.logical_not(edge) for edge in self.edges]

        @pl.when(low_t)
        def _():
            grid[0:1] = jnp.zeros(layer, f32)

        @pl.when(high_t)
        def _():
            grid[span - 1 : span] = jnp.zeros(layer, f32)

        @pl.when(low_h)
        def _():
            grid[:, 0:1] = jnp.zeros(column, f32)

        @pl.when(high_h)
        def _():
            grid[:, wide - 1 : wide] = jnp.zeros(column, f32)

    def inside(self, t, h):
        span, wide = self.grid.shape[0], self.grid.shape[1]
        low_t, high_t, low_h, high_h = self.edges
        conditions = []
        if t == 0:
            conditions.append(low_t)
        if t == span - 1:
            conditions.append(high_t)
        if h == 0:
            conditions.append(low_h)
        if h == wide - 1:
            conditions.append(high_h)
        if not conditions:
            return None
        result = conditions[0].astype(f32)
        for condition in conditions[1:]:
            result = result * condition.astype(f32)
        return result

    def inner(self):
        span, wide = self.grid.shape[0], self.grid.shape[1]
        return [(t, h) for t in range(1, span - 1) for h in range(1, wide - 1)]

    def rim(self):
        span, wide = self.grid.shape[0], self.grid.shape[1]
        inner = self.inner()
        return [(t, h) for t in range(span) for h in range(wide) if (t, h) not in inner]

    def start(self, which):
        for i in which:

            @pl.when(self.sends[i])
            def _(i=i):
                self.copies[i].start()

    def arrive(self, which):
        for i in which:

            @pl.when(self.receives[i])
            def _(i=i):
                self.copies[i].wait_recv()

    def begin(self):
        self.start((1, 3, 0, 2))

    def pass_on(self):
        self.arrive((1,))
        self.start((7, 6))
        self.arrive((0,))
        self.start((5, 4))

    def finish(self):
        self.arrive((2, 3, 4, 5, 6, 7))
        for i in range(8):

            @pl.when(self.sends[i])
            def _(i=i):
                self.copies[i].wait_send()


class Share:
    def __init__(self, place, slots, send, receive):
        self.place = place
        self.slots = slots
        mine = slots.at[pl.ds(place.index, 1)]
        self.copies = [
            remote(mine, mine, send.at[d - 1], receive.at[d - 1], place.other(d))
            for d in range(1, place.devices)
        ]

    def start(self, value):
        self.slots[pl.ds(self.place.index, 1)] = value[None]
        for copy in self.copies:
            copy.start()

    def finish(self):
        for copy in self.copies:
            copy.wait_recv()
        for copy in self.copies:
            copy.wait_send()
        return self.slots[...]


class Reduction:
    def __init__(self, place, values, landing, inbox, whole, base, rows, order, send, receive):
        self.values, self.landing, self.inbox, self.whole = values, landing, inbox, whole
        self.base, self.rows = base, rows
        self.send, self.receive = send, receive
        self.stage = 0
        self.pending = None
        self.partners = []
        for axis, bit in order:
            mine = place.tm if axis == "tm" else place.space
            digit = lax.rem(lax.div(mine, bit), 2)
            partner = mine + bit * (1 - 2 * digit)
            device = (partner, place.space) if axis == "tm" else (place.tm, partner)
            self.partners.append((digit, device))
        half = values.shape[1] // 2
        digit, _ = self.partners[0]
        self.columns = pl.ds(pl.multiple_of(digit * half, lanes), half)
        self.others = pl.ds(pl.multiple_of((1 - digit) * half, lanes), half)
        self.kept = (base, rows)
        self.regions = []
        self.slot = pl.ds(base, rows)
        self.free = base

    def span(self, region):
        start, size = region
        return pl.ds(pl.multiple_of(start, 8), size)

    def move(self, source, target, device):
        self.pending = remote(
            source, target, self.send.at[self.stage], self.receive.at[self.stage], device
        )
        self.pending.start()

    def take(self, size):
        self.slot = pl.ds(self.free, size)
        self.free += size
        return self.inbox.at[self.slot]

    def step(self):
        last = len(self.partners) - 1
        stage = self.stage
        if self.pending is not None:
            self.pending.wait()
            self.pending = None
        if stage == 0:
            rows = self.span(self.kept)
            self.move(self.values.at[rows, self.others], self.landing.at[rows], self.partners[0][1])
        elif stage <= last:
            rows = self.span(self.kept)
            source = self.landing if stage == 1 else self.inbox
            self.values[rows, self.columns] += source[self.slot]
            digit, device = self.partners[stage]
            start, size = self.kept
            if stage < last:
                half = size // 2
                self.regions.append(self.kept)
                self.kept = (start + digit * half, half)
                rows = self.span((start + (1 - digit) * half, half))
                size = half
            self.move(self.values.at[rows, self.columns], self.take(size), device)
        elif stage <= 2 * last:
            rows = self.span(self.kept)
            if stage == last + 1:
                self.whole[rows, self.columns] = self.values[rows, self.columns] + self.inbox[self.slot]
            region = self.whole.at[rows, self.columns]
            self.move(region, region, self.partners[2 * last - stage][1])
            if self.regions:
                self.kept = self.regions.pop()
        self.stage += 1


class KernelSum:
    def __init__(self, place, partial, pieces, rows_tm, whole, send, receive):
        self.place = place
        self.partial, self.pieces, self.rows_tm, self.whole = partial, pieces, rows_tm, whole
        n, m = place.size_space, place.size_tm
        size = pieces.shape[1]
        self.size = size
        mine = place.space

        def part(index):
            return partial.at[pl.ds(pl.multiple_of(index * size, 8), size)]

        self.own = part(mine)
        self.scatter = [
            remote(
                part(lax.rem(mine + d, n)),
                pieces.at[mine],
                send.at[d - 1],
                receive.at[d - 1],
                place.along_space(d),
            )
            for d in range(1, n)
        ]
        slot = rows_tm.at[place.tm]
        self.exchange = [
            remote(slot, slot, send.at[n - 2 + d], receive.at[n - 2 + d], place.along_tm(d))
            for d in range(1, m)
        ]
        slot = whole.at[mine]
        self.gather = [
            remote(slot, slot, send.at[n + m - 3 + d], receive.at[n + m - 3 + d], place.along_space(d))
            for d in range(1, n)
        ]

    def start(self, value):
        rows, total = value.shape[0], self.partial.shape[0]
        self.partial[0:rows] = value
        if total > rows:
            self.partial[rows:total] = jnp.zeros((total - rows, value.shape[1]), f32)
        for copy in self.scatter:
            copy.start()
        self.pieces[pl.ds(self.place.space, 1)] = self.own[...][None]

    def end(self, copies):
        for copy in copies:
            copy.wait_recv()
        for copy in copies:
            copy.wait_send()

    def across(self):
        self.end(self.scatter)
        total = added([self.pieces[i] for i in range(self.place.size_space)])
        self.rows_tm[pl.ds(self.place.tm, 1)] = total[None]
        for copy in self.exchange:
            copy.start()

    def back(self):
        self.end(self.exchange)
        total = added([self.rows_tm[i] for i in range(self.place.size_tm)])
        self.whole[pl.ds(self.place.space, 1)] = total[None]
        for copy in self.gather:
            copy.start()

    def finish(self):
        self.end(self.gather)


def added(parts):
    total = parts[0]
    for part in parts[1:]:
        total = total + part
    return total


def diagonal(shape):
    return lax.broadcasted_iota(jnp.int32, shape, 0) == lax.broadcasted_iota(jnp.int32, shape, 1)


def as_row(column, wide=lanes):
    shape = (column.shape[0], wide)
    return jnp.sum(jnp.where(diagonal(shape), jnp.broadcast_to(column, shape), 0.0), axis=0, keepdims=True)


def as_column(row, chans):
    shape = (chans, row.shape[1])
    return jnp.sum(jnp.where(diagonal(shape), jnp.broadcast_to(row, shape), 0.0), axis=1, keepdims=True)


def per_channel(values):
    return jnp.sum(added(values), axis=1, keepdims=True)


def local_moments(values):
    count = len(values) * values[0].shape[1]
    mean = per_channel(values) / count
    centered = [value - mean for value in values]
    squares = per_channel([value * value for value in centered])
    return jnp.concatenate([as_row(mean), as_row(squares)], axis=0)


def whole_moments(parts, count, chans):
    devices = parts.shape[0]
    means, squares = parts[:, 0:1], parts[:, 1:2]
    middle = jnp.sum(means, axis=0, keepdims=True) / devices
    offset = means - middle
    total = jnp.sum(squares + offset * offset * float(count), axis=0) / float(count * devices)
    return as_column(middle[0], chans), lax.rsqrt(as_column(total, chans) + eps)


def load_taps(kernel, taps, backward):
    chans = kernel.shape[3]
    taps[...] = jnp.zeros(taps.shape, f32)
    for a in range(3):
        for b in range(3):
            for e in range(3):
                tap = kernel[2 - a, 2 - b, 2 - e].T if backward else kernel[a, b, e]
                taps[(e * 3 + a) * 3 + b, :, 0:chans] = tap


def toeplitz(taps, high, low, rows):
    chans = taps.shape[1]
    high[...] = jnp.zeros(high.shape, bf16)
    low[...] = jnp.zeros(low.shape, bf16)
    size = rows * chans
    for e in range(3):
        for a in range(3):
            block = []
            for h in range(rows):
                parts = []
                for b in range(3):
                    tap = taps[(e * 3 + a) * 3 + b]
                    parts.append(pltpu.roll(tap, (h + b) * chans, 1) if h + b else tap)
                block.append(added(parts))
            top, bottom = halves(jnp.concatenate(block, axis=0))
            for t in range(2):
                place = (pl.ds((e * 2 + t) * size, size), pl.ds((t + a) * lanes, lanes))
                high[place] = top
                low[place] = bottom


def side_masks(shape, width):
    place = lax.rem(lax.broadcasted_iota(jnp.int32, shape, 1), width)
    return place > 0, place < width - 1


def later(value, inside):
    return jnp.where(inside, pltpu.roll(value, 1, 1), 0.0)


def earlier(value, inside):
    return jnp.where(inside, pltpu.roll(value, value.shape[1] - 1, 1), 0.0)


def convolve(high, low, grid_high, grid_low, rows, chans, width):
    depth = high.shape[1]
    size = 2 * rows * chans
    pairs = (grid_high.shape[0] - 2 * lanes) // (2 * lanes)
    result = []
    for pair in range(pairs):
        span = pl.ds(pair * 2 * lanes, depth)
        value = dot(high[...], grid_high[span])
        value = value + dot(high[...], grid_low[span])
        value = value + dot(low[...], grid_high[span])
        first, last = side_masks((size, value.shape[1]), width)
        result.append(
            later(value[0:size], first)
            + value[size : 2 * size]
            + earlier(value[2 * size : 3 * size], last)
        )
    flat = jnp.concatenate(result, axis=0)
    return [flat[i : i + chans] for i in range(0, flat.shape[0], chans)]


def kernel_gradient(grad, grid_high, grid_low, rows, width):
    chans = grad[0].shape[0]
    total = None
    for pair in range(len(grad) // (2 * rows)):
        block = jnp.concatenate(grad[2 * rows * pair : 2 * rows * (pair + 1)], axis=0)
        first, last = side_masks(block.shape, width)
        taps = jnp.concatenate([earlier(block, last), block, later(block, first)], axis=0)
        high, low = halves(taps)
        span = pl.ds(pair * 2 * lanes, 4 * lanes)
        value = dot_nt(high, grid_high[span])
        value = value + dot_nt(high, grid_low[span])
        value = value + dot_nt(low, grid_high[span])
        total = value if total is None else total + value
    half = rows * chans
    blocks = []
    for e in range(3):
        for a in range(3):
            block = added(
                [
                    total[(e * 2 + t) * half : (e * 2 + t + 1) * half, (t + a) * lanes : (t + a + 1) * lanes]
                    for t in range(2)
                ]
            )
            parts = [block[0:chans]]
            for h in range(1, rows):
                parts.append(pltpu.roll(block[h * chans : (h + 1) * chans], lanes - h * chans, 1))
            blocks.append(added(parts))
    return jnp.concatenate(blocks, axis=0)


class Loads:
    def __init__(self, pairs, semaphores):
        self.copies = [
            pltpu.make_async_copy(source, target, semaphores.at[i])
            for i, (source, target) in enumerate(pairs)
        ]

    def start(self, *which):
        for i in which:
            self.copies[i].start()

    def wait(self, *which):
        for i in which:
            self.copies[i].wait()


def forward_kernel(
    sizes,
    features,
    kernel_one,
    kernel_two,
    gain_one,
    shift_one,
    gain_two,
    shift_two,
    input_high_out,
    input_low_out,
    hidden_high_out,
    hidden_low_out,
    normed_one_out,
    normed_two_out,
    slope_one_out,
    slope_two_out,
    latent_out,
    pooled_out,
    scale_one,
    scale_two,
    grid_one,
    grid_two,
    grid_three,
    input_high,
    input_low,
    hidden_high,
    hidden_low,
    normed_one,
    normed_two,
    slope_one,
    slope_two,
    latent,
    pooled,
    taps,
    high,
    low,
    slots_one,
    slots_two,
    halo_send,
    halo_receive,
    share_send,
    share_receive,
    store_done,
):
    width, slab, rows, chans = sizes["width"], sizes["slab"], sizes["rows"], sizes["chans"]
    crops = features.shape[2]
    cells = crops * width
    count = slab * rows * cells
    wide = rows + 2
    place = Place(sizes)
    halos = [
        Halo(place, grid, halo_send.at[i], halo_receive.at[i])
        for i, grid in enumerate((grid_one, grid_two, grid_three))
    ]
    shares = [
        Share(place, slots, share_send.at[i], share_receive.at[i])
        for i, slots in enumerate((slots_one, slots_two))
    ]
    stores = Loads(
        [
            (input_high, input_high_out),
            (input_low, input_low_out),
            (hidden_high, hidden_high_out),
            (hidden_low, hidden_low_out),
            (normed_one, normed_one_out),
            (normed_two, normed_two_out),
            (slope_one, slope_one_out),
            (slope_two, slope_two_out),
            (latent, latent_out),
            (pooled, pooled_out),
        ],
        store_done,
    )
    inner, rim = halos[0].inner(), halos[0].rim()
    for halo in halos:
        halo.clear()
    for t in range(slab):
        for h in range(rows):
            for crop in range(crops):
                grid_one[t + 1, h + 1, :, crop * width : (crop + 1) * width] = features[t, h, crop]
    place.barrier()
    halos[0].begin()

    def keep(t, h, value, top, bottom):
        span = pl.ds((t * wide + h) * chans, chans)
        top[span], bottom[span] = halves(value)

    load_taps(kernel_one, taps.at[0], False)
    toeplitz(taps.at[0], high.at[0], low.at[0], rows)
    for t, h in inner:
        keep(t, h, grid_one[t, h], input_high, input_low)
    halos[0].pass_on()
    load_taps(kernel_two, taps.at[1], False)
    toeplitz(taps.at[1], high.at[1], low.at[1], rows)
    gains = [as_column(gain[...], chans) for gain in (gain_one, gain_two)]
    shifts = [as_column(shift[...], chans) for shift in (shift_one, shift_two)]
    halos[0].finish()
    for t, h in rim:
        keep(t, h, grid_one[t, h], input_high, input_low)
    stores.start(0, 1)

    values = convolve(high.at[0], low.at[0], input_high, input_low, rows, chans, width)
    shares[0].start(local_moments(values))
    for (t, h), value in zip(inner, values):
        grid_two[t, h] = value
    halos[1].begin()
    mean, scale = whole_moments(shares[0].finish(), count, chans)
    scale_one[...] = scale

    def first_layer(t, h):
        normed = (grid_two[t, h] - mean) * scale
        normed_one[t, h] = normed
        hidden, slope = softplus_parts(gains[0] * normed + shifts[0])
        inside = halos[1].inside(t, h)
        keep(t, h, hidden if inside is None else hidden * inside, hidden_high, hidden_low)
        return slope

    for t, h in inner:
        slope_one[t - 1, h - 1] = first_layer(t, h)
    halos[1].pass_on()
    stores.start(6)
    halos[1].finish()
    for t, h in rim:
        first_layer(t, h)
    stores.start(2, 3, 4)

    values = convolve(high.at[1], low.at[1], hidden_high, hidden_low, rows, chans, width)
    shares[1].start(local_moments(values))
    for (t, h), value in zip(inner, values):
        grid_three[t, h] = value
    halos[2].begin()
    mean, scale_again = whole_moments(shares[1].finish(), count, chans)
    scale_two[...] = scale_again

    def second_layer(t, h):
        normed = (grid_three[t, h] - mean) * scale_again
        normed_two[t, h] = normed
        return gains[1] * normed + shifts[1] + grid_one[t, h]

    for t, h in inner:
        value, slope = softplus_parts(second_layer(t, h))
        latent[t - 1, h - 1] = value
        slope_two[t - 1, h - 1] = slope
    halos[2].pass_on()
    stores.start(7)
    for t in range(slab // 2):
        pooled[t] = added([latent[2 * t + i, h] for i in range(2) for h in range(rows)])
    stores.start(9)
    halos[2].finish()
    for t, h in rim:
        value = second_layer(t, h)
        if t > 0 and h > 0:
            value, _ = softplus_parts(value)
            latent[t - 1, h - 1] = value * halos[2].inside(t, h)
    stores.start(5, 8)
    stores.wait(*range(10))


def query_kernel(
    sizes,
    latent,
    cells,
    cotangent,
    weight_one,
    bias_one,
    weight_two,
    bias_two,
    weight_three,
    bias_three,
    weight_four,
    bias_four,
    fields,
    grad_latent,
    grads,
    one,
    one_t,
    two,
    two_t,
    three,
    three_t,
    four,
    four_t,
    wide_two,
    wide_three,
    wide_four,
    pad_one,
    pad_four,
    along,
    plane,
    inputs,
    cot_pad,
    cot_sum,
    cots,
    grad_one,
    grad_four,
    grad_biases,
    h1,
    h2,
    h3,
    s1,
    s2,
    s3,
    g1,
    g2,
    g3,
    z_even,
    z_odd,
):
    crop = pl.program_id(0)
    slab, rows, width, chans = sizes["slab"], sizes["rows"], sizes["width"], sizes["chans"]
    hidden = weight_two.shape[0]
    queries = cells.shape[2]
    span_time, span_rows = slab + 1, rows + 1
    size_one, size_four = pad_one.shape[0], pad_four.shape[0]

    @pl.when(crop == 0)
    def _():
        known = weight_one.shape[0]
        pad_one[...] = jnp.zeros(pad_one.shape, f32)
        pad_one[0:known] = weight_one[...]
        pad_one[known : known + 1] = bias_one[...]
        pad_four[...] = jnp.zeros(pad_four.shape, f32)
        pad_four[0 : weight_four.shape[0]] = weight_four[...]
        for source, target in ((pad_one, one), (pad_four, four_t)):
            top, bottom = [part.astype(f32) for part in halves(source[...])]
            rest = target.shape[1] - 4 * source.shape[0]
            stack = [top, top, bottom, bottom, jnp.zeros((rest, hidden), f32)]
            target[...] = jnp.concatenate(stack, axis=0).T.astype(bf16)
        for source, target in ((pad_one[0:chans], one_t), (pad_four[...], four), (weight_two[...], two), (weight_three[...], three)):
            top, bottom = halves(source)
            target[0 : source.shape[0]] = top
            target[source.shape[0] :] = bottom
        for source, target in ((weight_two, two_t), (weight_three, three_t)):
            top, bottom = halves(source[...].T)
            target[0:hidden] = top
            target[hidden:] = bottom
        for source, target in ((bias_two, wide_two), (bias_three, wide_three)):
            column = jnp.broadcast_to(source[...], (lanes, hidden)).T
            for start in range(0, chunk, lanes):
                target[:, start : start + lanes] = column
        kind = lax.broadcasted_iota(jnp.int32, wide_four.shape, 0)
        bias = jnp.zeros(wide_four.shape, f32)
        for i in range(weight_four.shape[0]):
            bias = jnp.where(kind == i, bias_four[i], bias)
        wide_four[...] = bias
        inputs[...] = jnp.zeros(inputs.shape, bf16)
        cots[...] = jnp.zeros(cots.shape, bf16)
        for target in (cot_pad, cot_sum, grad_one, grad_four, grad_biases, grads):
            target[...] = jnp.zeros(target.shape, f32)

    @pl.when(lax.rem(crop, 2) == 0)
    def _():
        grad_latent[...] = jnp.zeros(grad_latent.shape, f32)

    def product(weights, values, span):
        both = dot(weights[...], values[0:hidden, span])
        return both[0:hidden] + both[hidden:] + dot(weights[0:hidden], values[hidden:, span])

    def keep(target, span, value):
        top, bottom = halves(value)
        target[0:hidden, span] = top
        target[hidden:, span] = bottom

    spans = [slice(start, start + chunk) for start in range(0, queries, chunk)]
    latent_parts = jnp.concatenate(halves(latent[...]), axis=1)
    cot_pad[0 : cotangent.shape[1]] = cotangent[0]
    cot_sum[...] += cot_pad[...]
    offset_time = lax.axis_index("tm") * slab
    offset_rows = lax.axis_index("space") * rows
    offset_width = lax.rem(crop, 2) * width

    for span in spans:
        time = cells[0, pl.ds(crop, 1), span]
        row = cells[1, pl.ds(crop, 1), span]
        place = cells[2, pl.ds(crop, 1), span]
        lane = lax.broadcasted_iota(jnp.int32, (lanes, chunk), 0)
        low = place + offset_width
        weights = jnp.where(lane == low, 1.0 - fraction_width, jnp.where(lane == low + 1, fraction_width, 0.0))
        weights = weights.astype(bf16)
        along[0:lanes, span] = weights
        along[lanes:, span] = weights
        values = dot(latent_parts, along[:, span])
        sampled = None
        for t in range(span_time):
            local = time - offset_time
            weight_time = jnp.where(local == t, 1.0 - fraction_time, jnp.where(local == t - 1, fraction_time, 0.0))
            for h in range(span_rows):
                local = row - offset_rows
                weight_rows = jnp.where(local == h, 1.0 - fraction_rows, jnp.where(local == h - 1, fraction_rows, 0.0))
                weight = weight_time * weight_rows
                index = t * span_rows + h
                plane[index : index + 1, span] = weight
                part = weight * values[index * chans : (index + 1) * chans]
                sampled = part if sampled is None else sampled + part
        coords = [
            2.0 * (time.astype(f32) + fraction_time) / sizes["depth"] - 1.0,
            2.0 * (row.astype(f32) + fraction_rows) / sizes["height"] - 1.0,
            2.0 * (place.astype(f32) + fraction_width) / width - 1.0,
        ]
        kind = lax.broadcasted_iota(jnp.int32, (size_one - chans, chunk), 0)
        extra = jnp.where(kind == 3, 1.0, 0.0)
        for i, coord in enumerate(coords):
            extra = jnp.where(kind == i, coord, extra)
        top, bottom = halves(jnp.concatenate([sampled, extra], axis=0))
        size = top.shape[0]
        for i, part in enumerate((top, bottom, top, bottom)):
            inputs[i * size : (i + 1) * size, span] = part
        top, bottom = halves(cot_pad[:, span])
        size = top.shape[0]
        for i, part in enumerate((top, bottom, top, bottom)):
            cots[i * size : (i + 1) * size, span] = part

    buffers = (z_even, z_odd)
    pending = []
    turn = [0]

    def emit(ahead, after=None):
        buffer = buffers[turn[0] % 2]
        turn[0] += 1
        ahead(buffer)
        flush()
        if after is not None:
            pending.append(lambda: after(buffer))

    def flush():
        while pending:
            pending.pop()()

    def forward(kept, slope_kept, span, bias):
        def after(buffer):
            value = buffer[...] if bias is None else buffer[...] + bias[...]
            value, slope = softplus_parts(value)
            keep(kept, span, value)
            slope_kept[:, span] = slope

        return after

    def backward(kept, slope_kept, span, bias):
        def after(buffer):
            grad = buffer[...] * slope_kept[:, span]
            keep(kept, span, grad)
            if bias is not None:
                grad_biases[bias] += added([grad[:, i : i + lanes] for i in range(0, chunk, lanes)])

        return after

    def store(make):
        def ahead(buffer):
            buffer[...] = make()

        return ahead

    def outer_part(start, grads_here, values, part):
        def ahead(buffer):
            rows_here = slice(part * chunk, (part + 1) * chunk)
            both = dot_nt(grads_here[...], values[rows_here])
            low = slice(hidden + part * chunk, hidden + (part + 1) * chunk)
            total = both[0:hidden] + both[hidden:] + dot_nt(grads_here[0:hidden], values[low])
            grads[start : start + hidden, rows_here] += total

        return ahead

    def fields_part(span):
        def ahead(buffer):
            both = dot(four[...], h3[0:hidden, span])
            value = both[0:size_four] + both[size_four:] + dot(four[0:size_four], h3[hidden:, span])
            fields[0, :, span] = (value + wide_four[...])[0 : fields.shape[1]]

        return ahead

    def grad_four_part(buffer):
        grad_four[...] += dot_nt(h3[0:hidden], cots[...]) + dot_nt(h3[hidden:], cots[...])

    def grad_one_part(buffer):
        grad_one[...] += dot_nt(g1[0:hidden], inputs[0:lanes]) + dot_nt(g1[hidden:], inputs[0:lanes])

    def latent_part(span):
        def ahead(buffer):
            both = dot(one_t[...], g1[0:hidden, span])
            buffer[0:chans] = both[0:chans] + both[chans:] + dot(one_t[0:chans], g1[hidden:, span])

        def after(buffer):
            grad = buffer[0:chans]
            spread = [plane[i : i + 1, span] * grad for i in range(span_time * span_rows)]
            top, bottom = halves(jnp.concatenate(spread, axis=0))
            grad_latent[...] += dot_nt(top, along[0:lanes, span]) + dot_nt(bottom, along[0:lanes, span])

        return ahead, after

    parts = hidden // chunk
    for span in spans:
        emit(store(lambda: dot(one[...], inputs[:, span])), forward(h1, s1, span, None))
    for span in spans:
        emit(store(lambda: product(two, h1, span)), forward(h2, s2, span, wide_two))
    for span in spans:
        emit(store(lambda: product(three, h2, span)), forward(h3, s3, span, wide_three))
    for span in spans:
        emit(store(lambda: dot(four_t[...], cots[:, span])), backward(g3, s3, span, 1))
        emit(fields_part(span))
    emit(grad_four_part)
    for span in spans:
        emit(store(lambda: product(three_t, g3, span)), backward(g2, s2, span, 0))
    for part in range(parts):
        emit(outer_part(hidden, g3, h2, part))
    for span in spans:
        emit(store(lambda: product(two_t, g2, span)), backward(g1, s1, span, None))
    outers = [outer_part(0, g2, h1, part) for part in range(parts)]
    for i, span in enumerate(spans):
        emit(*latent_part(span))
        if i % 2 and outers:
            emit(outers.pop(0))
    for rest in outers:
        emit(rest)
    emit(grad_one_part)
    flush()

    @pl.when(crop == pl.num_programs(0) - 1)
    def _():
        start = 2 * hidden
        for source, size in ((grad_one, size_one), (grad_four, size_four)):
            flat = source[...].T
            grads[start : start + size] = flat[0:size] + flat[size : 2 * size]
            start += size
        for i in range(2):
            grads[start + i : start + i + 1] = jnp.sum(grad_biases[i].T, axis=0, keepdims=True)
        total = jnp.sum(cot_sum[...], axis=1, keepdims=True)
        grads[start + 2 : start + 3] = as_row(total, hidden)


def backward_kernel(
    sizes,
    grad_latent_in,
    upsampled_in,
    input_high_in,
    input_low_in,
    hidden_high_in,
    hidden_low_in,
    normed_one_in,
    normed_two_in,
    slope_one_in,
    slope_two_in,
    grads_in,
    scale_one,
    scale_two,
    gain_one,
    gain_two,
    kernel_one,
    kernel_two,
    grad_features,
    grads_out,
    grad_kernels,
    sums,
    folded,
    upsampled,
    input_high,
    input_low,
    hidden_high,
    hidden_low,
    normed_one,
    normed_two,
    slope_one,
    slope_two,
    grads,
    landing,
    inbox,
    whole,
    arrived_time,
    arrived_rows,
    grid_one,
    grid_two,
    grid_high,
    grid_low,
    grad_summed,
    taps,
    high,
    low,
    partial,
    pieces,
    rows_tm,
    gathered,
    slots_one,
    slots_two,
    halo_send,
    halo_receive,
    share_send,
    share_receive,
    sum_send,
    sum_receive,
    reduce_send,
    reduce_receive,
    load_done,
):
    width, slab, rows, chans = sizes["width"], sizes["slab"], sizes["rows"], sizes["chans"]
    wide = rows + 2
    cells = upsampled.shape[2]
    crops = cells // width
    place = Place(sizes)
    count = float(slab * rows * cells * place.devices)
    halo_one = Halo(place, grid_one, halo_send.at[0], halo_receive.at[0])
    halo_two = Halo(place, grid_two, halo_send.at[1], halo_receive.at[1])
    share_one = Share(place, slots_one, share_send.at[0], share_receive.at[0])
    share_two = Share(place, slots_two, share_send.at[1], share_receive.at[1])
    kernel_sums = [
        KernelSum(
            place,
            partial.at[i],
            pieces.at[i],
            rows_tm.at[i],
            gathered.at[i],
            sum_send.at[i],
            sum_receive.at[i],
        )
        for i in range(2)
    ]
    bits_tm = [("tm", 1 << i) for i in range(place.size_tm.bit_length() - 1)]
    bits_space = [("space", 1 << i) for i in range(place.size_space.bit_length() - 1)]
    orders = [
        [bits_space[0]] + bits_tm[1:] + bits_space[1:] + bits_tm[:1],
        bits_space + bits_tm[1:] + bits_tm[:1],
    ]
    half = grads.shape[0] // 2
    reductions = [
        Reduction(
            place,
            grads,
            landing,
            inbox,
            whole,
            i * half,
            half,
            orders[i],
            reduce_send.at[i],
            reduce_receive.at[i],
        )
        for i in range(2)
    ]
    total_steps = 2 * len(orders[0])

    def reduce_step():
        for reduction in reductions:
            if reduction.stage < total_steps:
                reduction.step()

    loads = Loads(
        [
            (grad_latent_in, folded),
            (grads_in, grads),
            (upsampled_in, upsampled),
            (slope_two_in, slope_two),
            (normed_two_in, normed_two),
            (hidden_high_in, hidden_high),
            (hidden_low_in, hidden_low),
            (slope_one_in, slope_one),
            (normed_one_in, normed_one),
            (input_high_in, input_high),
            (input_low_in, input_low),
        ],
        load_done,
    )
    loads.start(*range(11))
    halo_one.clear()
    halo_two.clear()
    up_t, up_h = place.along_tm(1), place.along_space(1)
    low_t, high_t = place.tm > 0, place.tm < place.size_tm - 1
    low_h, high_h = place.space > 0, place.space < place.size_space - 1

    @pl.when(jnp.logical_not(low_t))
    def _():
        arrived_time[...] = jnp.zeros(arrived_time.shape, f32)

    @pl.when(jnp.logical_not(low_h))
    def _():
        arrived_rows[...] = jnp.zeros(arrived_rows.shape, f32)

    send, receive = halo_send.at[2], halo_receive.at[2]
    time_copy = remote(folded.at[pl.ds(slab, 1)], arrived_time, send.at[0], receive.at[0], up_t)
    rows_copy = remote(
        folded.at[pl.ds(1, slab - 1), pl.ds(rows, 1)],
        arrived_rows.at[pl.ds(1, slab - 1)],
        send.at[1],
        receive.at[1],
        up_h,
    )
    corner_copy = remote(
        folded.at[pl.ds(0, 1), pl.ds(rows, 1)],
        arrived_rows.at[pl.ds(0, 1)],
        send.at[2],
        receive.at[2],
        up_h,
    )
    loads.wait(0)
    place.barrier()

    @pl.when(high_t)
    def _():
        time_copy.start()

    @pl.when(high_h)
    def _():
        rows_copy.start()

    loads.wait(1)
    reduce_step()
    load_taps(kernel_two, taps.at[1], True)
    toeplitz(taps.at[1], high.at[1], low.at[1], rows)
    gains = [as_column(gain[...], chans) for gain in (gain_one, gain_two)]

    @pl.when(low_t)
    def _():
        time_copy.wait_recv()

    folded[0:1] += arrived_time[...]

    @pl.when(high_h)
    def _():
        corner_copy.start()

    reduce_step()
    load_taps(kernel_one, taps.at[0], True)
    toeplitz(taps.at[0], high.at[0], low.at[0], rows)

    @pl.when(low_h)
    def _():
        rows_copy.wait_recv()
        corner_copy.wait_recv()

    @pl.when(high_t)
    def _():
        time_copy.wait_send()

    @pl.when(high_h)
    def _():
        rows_copy.wait_send()
        corner_copy.wait_send()

    folded[0:slab, 0:1] += arrived_rows[...]
    loads.wait(2, 3, 4)
    reduce_step()

    inner, rim = halo_one.inner(), halo_one.rim()

    def norm_sums(grads_here, normed):
        cross = [grad * normed[t, h] for (t, h), grad in zip(inner, grads_here)]
        return jnp.concatenate(
            [as_row(per_channel(grads_here)), as_row(per_channel(cross))], axis=0
        )

    def norm_terms(parts, scale, gain):
        result = jnp.sum(parts, axis=0)
        total = as_column(result[0:1], chans) / count
        cross = as_column(result[1:2], chans) / count
        return result, total, cross, gain * scale[...]

    def keep(t, h, value):
        span = pl.ds((t * wide + h) * chans, chans)
        grid_high[span], grid_low[span] = halves(value)

    values = []
    for t, h in inner:
        value = folded[t - 1, h - 1] + upsampled[(t - 1) // 2]
        value = value * slope_two[t - 1, h - 1]
        grad_summed[t - 1, h - 1] = value
        grid_two[t, h] = value
        values.append(value)
    share_two.start(norm_sums(values, normed_two))
    halo_two.begin()
    result, total, cross, factor = norm_terms(share_two.finish(), scale_two, gains[1])
    sums[1] = result
    reduce_step()
    values = []
    for t, h in inner:
        value = factor * (grid_two[t, h] - total - normed_two[t, h] * cross)
        values.append(value)
        keep(t, h, value)
    halo_two.pass_on()
    loads.wait(5, 6)
    kernel_sums[1].start(kernel_gradient(values, hidden_high, hidden_low, rows, width))
    halo_two.finish()
    for t, h in rim:
        value = factor * (grid_two[t, h] - total - normed_two[t, h] * cross)
        keep(t, h, value * halo_two.inside(t, h))
    reduce_step()
    loads.wait(7, 8)
    values = convolve(high.at[1], low.at[1], grid_high, grid_low, rows, chans, width)
    values = [value * slope_one[t - 1, h - 1] for (t, h), value in zip(inner, values)]
    share_one.start(norm_sums(values, normed_one))
    for (t, h), value in zip(inner, values):
        grid_one[t, h] = value
    halo_one.begin()
    kernel_sums[1].across()
    reduce_step()
    result, total, cross, factor = norm_terms(share_one.finish(), scale_one, gains[0])
    sums[0] = result
    values = []
    for t, h in inner:
        value = factor * (grid_one[t, h] - total - normed_one[t, h] * cross)
        values.append(value)
        keep(t, h, value)
    halo_one.pass_on()
    kernel_sums[1].back()
    loads.wait(9, 10)
    kernel_sums[0].start(kernel_gradient(values, input_high, input_low, rows, width))
    reduce_step()
    halo_one.finish()
    for t, h in rim:
        value = factor * (grid_one[t, h] - total - normed_one[t, h] * cross)
        keep(t, h, value * halo_one.inside(t, h))
    reduce_step()
    values = convolve(high.at[0], low.at[0], grid_high, grid_low, rows, chans, width)
    kernel_sums[0].across()
    reduce_step()
    for (t, h), value in zip(inner, values):
        value = value + grad_summed[t - 1, h - 1]
        for crop in range(crops):
            grad_features[t - 1, h - 1, crop] = value[:, crop * width : (crop + 1) * width]
    kernel_sums[0].back()
    while reductions[0].stage < total_steps:
        reduce_step()
    grads_out[...] = whole[...]
    for i in range(2):
        kernel_sums[i].finish()
        size = grad_kernels.shape[1]
        grad_kernels[i] = gathered[i].reshape(-1, lanes)[0:size]


def closing_kernel(
    sizes,
    grads,
    grad_kernels,
    sums,
    kernel_one,
    gain_one,
    shift_one,
    kernel_two,
    gain_two,
    shift_two,
    one,
    bias_one,
    two,
    bias_two,
    three,
    bias_three,
    four,
    bias_four,
):
    chans = sizes["chans"]
    hidden = two.shape[0]
    for i, kernel in enumerate((kernel_one, kernel_two)):
        for e in range(3):
            for a in range(3):
                block = grad_kernels[i, (e * 3 + a) * chans : (e * 3 + a + 1) * chans]
                for b in range(3):
                    kernel[a, b, e] = block[:, b * chans : (b + 1) * chans]
    for i, (gain, shift) in enumerate(((gain_one, shift_one), (gain_two, shift_two))):
        shift[...] = sums[i, 0:1, 0:chans]
        gain[...] = sums[i, 1:2, 0:chans]
    two[...] = grads[0:hidden]
    three[...] = grads[hidden : 2 * hidden]
    start = 2 * hidden
    known = one.shape[0]
    one[...] = grads[start : start + known]
    bias_one[...] = grads[start + known : start + known + 1]
    start += sizes["rows_one"]
    four[...] = grads[start : start + four.shape[0]]
    start += sizes["rows_four"]
    bias_two[...] = grads[start : start + 1]
    bias_three[...] = grads[start + 1 : start + 2]
    bias_four[...] = grads[start + 2 : start + 3, 0 : bias_four.shape[1]]


def in_vmem(count):
    return [pl.BlockSpec(memory_space=VMEM)] * count


def anywhere(count):
    return [pl.BlockSpec(memory_space=pl.ANY)] * count


def struct(shape, dtype=f32):
    return jax.ShapeDtypeStruct(shape, dtype)


def scratch(structs):
    return [VMEM(item.shape, item.dtype) for item in structs]


def per_device(
    mesh_sizes,
    features,
    conv_first,
    gain_first,
    shift_first,
    conv_second,
    gain_second,
    shift_second,
    weight_one,
    bias_one,
    weight_two,
    bias_two,
    weight_three,
    bias_three,
    weight_four,
    bias_four,
    query_cells,
    field_cotangent,
    pooled_cotangent,
):
    crops, chans, slab, rows, width = features.shape
    queries = query_cells.shape[2]
    hidden, known = weight_one.shape
    field_count = weight_four.shape[0]
    size_tm, size_space = mesh_sizes
    devices = size_tm * size_space
    cells = crops * width
    rows_one = -(-(known + 1) // 16) * 16
    rows_four = 16
    sizes = {
        "tm": size_tm,
        "space": size_space,
        "slab": slab,
        "rows": rows,
        "width": width,
        "chans": chans,
        "depth": slab * size_tm,
        "height": rows * size_space,
        "rows_one": rows_one,
        "rows_four": rows_four,
    }
    span, wide = slab + 2, rows + 2
    matrix = (2, 6 * rows * chans, 4 * wide * chans)
    taps = VMEM((2, 27, chans, lanes), f32)
    memory = pltpu.CompilerParams(vmem_limit_bytes=56 * 2**20)

    grid = jnp.transpose(features, (2, 3, 0, 1, 4))
    kernels = [jnp.transpose(kernel, (2, 3, 4, 0, 1)) for kernel in (conv_first, conv_second)]
    gains = [gain_first[None], gain_second[None]]
    shifts = [shift_first[None], shift_second[None]]
    block = struct((slab, rows, chans, cells))
    padded = struct((span, wide, chans, cells))
    flat = struct((span * wide * chans, cells), bf16)
    column = struct((chans, 1))
    slots = VMEM((devices, 2, lanes), f32)
    kept = [flat] * 4 + [padded] * 2 + [block] * 2
    kept += [struct((slab + 1, rows + 1, chans, cells)), struct((slab // 2, chans, cells))]
    copies = pltpu.SemaphoreType.DMA
    (
        input_high,
        input_low,
        hidden_high,
        hidden_low,
        normed_one,
        normed_two,
        slope_one,
        slope_two,
        latent,
        pool_part,
        scale_one,
        scale_two,
    ) = pl.pallas_call(
        functools.partial(forward_kernel, sizes),
        out_shape=kept + [column] * 2,
        in_specs=in_vmem(7),
        out_specs=anywhere(10) + in_vmem(2),
        scratch_shapes=[
            *scratch([padded] * 3 + kept),
            taps,
            VMEM(matrix, bf16),
            VMEM(matrix, bf16),
            slots,
            slots,
            copies((3, 8)),
            copies((3, 8)),
            copies((2, devices - 1)),
            copies((2, devices - 1)),
            copies((10,)),
        ],
        compiler_params=pltpu.CompilerParams(
            collective_id=0, has_side_effects=True, vmem_limit_bytes=56 * 2**20
        ),
        name="forward_block",
    )(grid, *kernels, gains[0], shifts[0], gains[1], shifts[1])
    pooled = pool_part.reshape(slab // 2, chans, crops, width // 2, 2).sum(axis=4) * (0.25 / rows)
    pooled = jnp.transpose(pooled, (2, 1, 0, 3))[:, :, :, None, :]

    sample_rows = (slab + 1) * (rows + 1)
    unit = 8 << (devices.bit_length() - 3)
    reduce_rows = -(-(2 * hidden + rows_one + rows_four + 8) // (2 * unit)) * 2 * unit
    pair_block = pl.BlockSpec((sample_rows * chans, lanes), lambda n: (0, n // 2))
    crop_block = pl.BlockSpec((1, field_count, queries), lambda n: (n, 0, 0))

    def constant(shape):
        return pl.BlockSpec(shape, lambda n: (0,) * len(shape))

    operands = [
        latent.reshape(sample_rows * chans, cells),
        query_cells,
        jnp.transpose(field_cotangent, (1, 0, 2)),
        jnp.transpose(weight_one),
        bias_one[None],
        weight_two,
        bias_two[None],
        weight_three,
        bias_three[None],
        weight_four,
        bias_four,
    ]
    specs = [pair_block, constant(query_cells.shape), crop_block]
    specs += [constant(operand.shape) for operand in operands[3:-1]]
    specs += [pl.BlockSpec(memory_space=pltpu.SMEM)]
    outs = [
        struct((crops, field_count, queries)),
        struct((sample_rows * chans, cells)),
        struct((reduce_rows, hidden)),
    ]
    fields, grad_latent, grads = pl.pallas_call(
        functools.partial(query_kernel, sizes),
        grid=(crops,),
        out_shape=outs,
        in_specs=specs,
        out_specs=[crop_block, pair_block, constant(outs[2].shape)],
        scratch_shapes=[
            VMEM((hidden, 256), bf16),
            VMEM((2 * chans, hidden), bf16),
            *[VMEM((2 * hidden, hidden), bf16)] * 4,
            VMEM((2 * rows_four, hidden), bf16),
            VMEM((hidden, lanes), bf16),
            VMEM((hidden, chunk), f32),
            VMEM((hidden, chunk), f32),
            VMEM((rows_four, chunk), f32),
            VMEM((rows_one, hidden), f32),
            VMEM((rows_four, hidden), f32),
            VMEM((2 * lanes, queries), bf16),
            VMEM((-(-sample_rows // 8) * 8, queries), f32),
            VMEM((256, queries), bf16),
            VMEM((rows_four, queries), f32),
            VMEM((rows_four, queries), f32),
            VMEM((lanes, queries), bf16),
            VMEM((hidden, lanes), f32),
            VMEM((hidden, lanes), f32),
            VMEM((2, hidden, lanes), f32),
            *[VMEM((2 * hidden, queries), bf16)] * 3,
            *[VMEM((hidden, queries), f32)] * 3,
            *[VMEM((2 * hidden, queries), bf16)] * 3,
            *[VMEM((hidden, chunk), f32)] * 2,
        ],
        compiler_params=pltpu.CompilerParams(
            dimension_semantics=("arbitrary",), vmem_limit_bytes=56 * 2**20
        ),
        name="query_network",
    )(*operands)

    upsampled = jnp.transpose(pooled_cotangent[:, :, :, 0], (2, 1, 0, 3)) * (0.25 / rows)
    upsampled = jnp.broadcast_to(upsampled[..., None], upsampled.shape + (2,))
    upsampled = upsampled.reshape(slab // 2, chans, cells)
    kernel_rows = 9 * chans
    piece = -(-kernel_rows // (8 * size_space)) * 8
    sum_copies = 2 * size_space + size_tm - 3
    reduce_block = struct((reduce_rows, hidden))
    half_block = struct((reduce_rows, hidden // 2))
    loaded = [struct((slab + 1, rows + 1, chans, cells)), struct((slab // 2, chans, cells))]
    loaded += [flat] * 4 + [padded] * 2 + [block] * 2 + [reduce_block]
    grad_features, grads, grad_kernels, sums = pl.pallas_call(
        functools.partial(backward_kernel, sizes),
        out_shape=[
            struct((slab, rows, crops, chans, width)),
            reduce_block,
            struct((2, kernel_rows, lanes)),
            struct((2, 2, lanes)),
        ],
        in_specs=anywhere(11) + in_vmem(6),
        out_specs=in_vmem(4),
        scratch_shapes=[
            *scratch(loaded),
            *scratch([half_block] * 2 + [reduce_block]),
            VMEM((1, rows + 1, chans, cells), f32),
            VMEM((slab, 1, chans, cells), f32),
            *scratch([padded] * 2 + [flat] * 2 + [block]),
            taps,
            VMEM(matrix, bf16),
            VMEM(matrix, bf16),
            VMEM((2, size_space * piece, lanes), f32),
            VMEM((2, size_space, piece, lanes), f32),
            VMEM((2, size_tm, piece, lanes), f32),
            VMEM((2, size_space, piece, lanes), f32),
            slots,
            slots,
            copies((3, 8)),
            copies((3, 8)),
            copies((2, devices - 1)),
            copies((2, devices - 1)),
            copies((2, sum_copies)),
            copies((2, sum_copies)),
            copies((2, 2 * devices.bit_length())),
            copies((2, 2 * devices.bit_length())),
            copies((11,)),
        ],
        compiler_params=pltpu.CompilerParams(
            collective_id=1, has_side_effects=True, vmem_limit_bytes=56 * 2**20
        ),
        name="backward_block",
    )(
        grad_latent.reshape(slab + 1, rows + 1, chans, cells),
        upsampled,
        input_high,
        input_low,
        hidden_high,
        hidden_low,
        normed_one,
        normed_two,
        slope_one,
        slope_two,
        grads,
        scale_one,
        scale_two,
        gains[0],
        gains[1],
        *kernels,
    )
    row = struct((1, chans))
    wide_row = struct((1, hidden))
    taps_shape = struct((3, 3, 3, chans, chans))
    closing = pl.pallas_call(
        functools.partial(closing_kernel, sizes),
        out_shape=[
            taps_shape,
            row,
            row,
            taps_shape,
            row,
            row,
            struct((known, hidden)),
            wide_row,
            struct((hidden, hidden)),
            wide_row,
            struct((hidden, hidden)),
            wide_row,
            struct((field_count, hidden)),
            struct((1, field_count)),
        ],
        in_specs=in_vmem(3),
        out_specs=in_vmem(14),
        compiler_params=memory,
        name="closing",
    )(grads, grad_kernels, sums)
    closing = list(closing)
    for i in (0, 3):
        closing[i] = jnp.transpose(closing[i], (3, 4, 0, 1, 2))
    closing[6] = jnp.transpose(closing[6])
    for i in (1, 2, 4, 5, 7, 9, 11, 13):
        closing[i] = closing[i][0]
    return (
        jnp.transpose(fields, (1, 0, 2)),
        pooled,
        jnp.transpose(grad_features, (2, 3, 0, 1, 4)),
        *closing,
    )


def solution(mesh):
    placed = (P(None, None, "tm", "space", None),) + (P(),) * 14
    placed += (P(None, None, ("tm", "space")),) * 2 + (P(None, None, "tm", "space", None),)
    return jax.shard_map(
        functools.partial(per_device, (mesh.shape["tm"], mesh.shape["space"])),
        mesh=mesh,
        in_specs=placed,
        out_specs=(
            P(None, None, ("tm", "space")),
            P(None, None, "tm", "space", None),
            P(None, None, "tm", "space", None),
        )
        + (P(),) * 14,
        check_vma=False,
    )
```

```python
import functools

import jax
import jax.numpy as jnp
from jax import lax
from jax.experimental import pallas as pl
from jax.experimental.pallas import tpu as pltpu
from jax.sharding import PartitionSpec as P

MESH = pl.DeviceIdType.MESH
VMEM = pltpu.VMEM
f32 = jnp.float32
bf16 = jnp.bfloat16
f8 = jnp.float8_e4m3fn

eps = 1e-05
fraction_time = 0.25
fraction_rows = 0.5
fraction_width = 0.75
chunk = 256
lanes = 128


def dot(a, b):
    return lax.dot_general(a, b, (((1,), (0,)), ((), ())), preferred_element_type=f32)


def dot_nt(a, b):
    return lax.dot_general(a, b, (((1,), (1,)), ((), ())), preferred_element_type=f32)


def halves(value):
    high = value.astype(bf16)
    return high, (value - high.astype(f32)).astype(bf16)


def split(value):
    high = value.astype(bf16)
    return high, value - high.astype(f32)


def softplus_parts(value):
    result = jnp.maximum(value, 0.0) + jnp.log(1.0 + jnp.exp(-jnp.abs(value)))
    return result, jnp.exp(value - result)


class Place:
    def __init__(self, sizes):
        self.size_tm = sizes["tm"]
        self.size_space = sizes["space"]
        self.devices = self.size_tm * self.size_space
        self.tm = lax.axis_index("tm")
        self.space = lax.axis_index("space")
        self.index = self.tm * self.size_space + self.space

    def along_tm(self, distance):
        return (lax.rem(self.tm + distance, self.size_tm), self.space)

    def along_space(self, distance):
        return (self.tm, lax.rem(self.space + distance, self.size_space))

    def other(self, distance):
        index = lax.rem(self.index + distance, self.devices)
        return (lax.div(index, self.size_space), lax.rem(index, self.size_space))

    def barrier(self):
        semaphore = pltpu.get_barrier_semaphore()
        for distance in range(1, self.devices):
            pl.semaphore_signal(
                semaphore, inc=1, device_id=self.other(distance), device_id_type=MESH
            )
        pl.semaphore_wait(semaphore, self.devices - 1)


def remote(source, target, send, receive, device):
    return pltpu.make_async_remote_copy(
        src_ref=source,
        dst_ref=target,
        send_sem=send,
        recv_sem=receive,
        device_id=device,
        device_id_type=MESH,
    )


class Halo:
    def __init__(self, place, grid, groups, send, receive):
        span, wide = grid.shape[0], grid.shape[1]
        top, side = span - 1, wide - 1
        inner_t, inner_h = pl.ds(1, span - 2), pl.ds(1, wide - 2)
        up_t, down_t = place.along_tm(1), place.along_tm(place.size_tm - 1)
        up_h, down_h = place.along_space(1), place.along_space(place.size_space - 1)
        low_t, high_t = place.tm > 0, place.tm < place.size_tm - 1
        low_h, high_h = place.space > 0, place.space < place.size_space - 1

        def one(index):
            return pl.ds(index, 1)

        both = jnp.logical_and
        table = [
            (high_t, low_t, (one(top - 1), inner_h), (one(0), inner_h), up_t),
            (low_t, high_t, (one(1), inner_h), (one(top), inner_h), down_t),
            (high_h, low_h, (inner_t, one(side - 1)), (inner_t, one(0)), up_h),
            (low_h, high_h, (inner_t, one(1)), (inner_t, one(side)), down_h),
            (both(high_h, low_t), both(low_h, low_t), (one(0), one(side - 1)), (one(0), one(0)), up_h),
            (both(low_h, low_t), both(high_h, low_t), (one(0), one(1)), (one(0), one(side)), down_h),
            (both(high_h, high_t), both(low_h, high_t), (one(top), one(side - 1)), (one(top), one(0)), up_h),
            (both(low_h, high_t), both(high_h, high_t), (one(top), one(1)), (one(top), one(side)), down_h),
        ]
        self.sends = [entry[0] for entry in table]
        self.receives = [entry[1] for entry in table]
        self.copies = []
        for number, group in enumerate(groups):
            part = (slice(None), group)
            self.copies.append(
                [
                    remote(
                        grid.at[entry[2] + part],
                        grid.at[entry[3] + part],
                        send.at[number, i],
                        receive.at[number, i],
                        entry[4],
                    )
                    for i, entry in enumerate(table)
                ]
            )
        self.grid = grid
        self.edges = (low_t, high_t, low_h, high_h)

    def clear(self):
        grid = self.grid
        span, wide = grid.shape[0], grid.shape[1]
        layer, column = (1,) + grid.shape[1:], (span, 1) + grid.shape[2:]
        low_t, high_t, low_h, high_h = [jnp.logical_not(edge) for edge in self.edges]

        @pl.when(low_t)
        def _():
            grid[0:1] = jnp.zeros(layer, f32)

        @pl.when(high_t)
        def _():
            grid[span - 1 : span] = jnp.zeros(layer, f32)

        @pl.when(low_h)
        def _():
            grid[:, 0:1] = jnp.zeros(column, f32)

        @pl.when(high_h)
        def _():
            grid[:, wide - 1 : wide] = jnp.zeros(column, f32)

    def inside(self, t, h):
        span, wide = self.grid.shape[0], self.grid.shape[1]
        low_t, high_t, low_h, high_h = self.edges
        conditions = []
        if t == 0:
            conditions.append(low_t)
        if t == span - 1:
            conditions.append(high_t)
        if h == 0:
            conditions.append(low_h)
        if h == wide - 1:
            conditions.append(high_h)
        if not conditions:
            return None
        result = conditions[0].astype(f32)
        for condition in conditions[1:]:
            result = result * condition.astype(f32)
        return result

    def inner(self):
        span, wide = self.grid.shape[0], self.grid.shape[1]
        return [(t, h) for t in range(1, span - 1) for h in range(1, wide - 1)]

    def rim(self):
        span, wide = self.grid.shape[0], self.grid.shape[1]
        inner = self.inner()
        return [(t, h) for t in range(span) for h in range(wide) if (t, h) not in inner]

    def start(self, group, which):
        for i in which:

            @pl.when(self.sends[i])
            def _(i=i):
                self.copies[group][i].start()

    def arrive(self, group, which):
        for i in which:

            @pl.when(self.receives[i])
            def _(i=i):
                self.copies[group][i].wait_recv()

    def begin(self):
        for group in range(len(self.copies)):
            self.start(group, (1, 3, 0, 2))

    def pass_on(self, group):
        if group < len(self.copies):
            self.arrive(group, (1,))
            self.start(group, (7, 6))
            self.arrive(group, (0,))
            self.start(group, (5, 4))

    def finish(self, group):
        self.arrive(group, (2, 3, 4, 5, 6, 7))

    def sent(self):
        for i in range(8):

            @pl.when(self.sends[i])
            def _(i=i):
                for copies in self.copies:
                    copies[i].wait_send()


class Share:
    def __init__(self, place, slots, send, receive):
        self.place = place
        self.slots = slots
        mine = slots.at[pl.ds(place.index, 1)]
        self.copies = [
            remote(mine, mine, send.at[d - 1], receive.at[d - 1], place.other(d))
            for d in range(1, place.devices)
        ]

    def start(self, value):
        self.slots[pl.ds(self.place.index, 1)] = value[None]
        for copy in self.copies:
            copy.start()

    def finish(self):
        for copy in self.copies:
            copy.wait_recv()
        for copy in self.copies:
            copy.wait_send()
        return self.slots[...]


class Reduction:
    def __init__(self, place, values, landing, inbox, whole, base, rows, order, send, receive):
        self.values, self.landing, self.inbox, self.whole = values, landing, inbox, whole
        self.base, self.rows = base, rows
        self.send, self.receive = send, receive
        self.stage = 0
        self.pending = None
        self.partners = []
        for axis, bit in order:
            mine = place.tm if axis == "tm" else place.space
            digit = lax.rem(lax.div(mine, bit), 2)
            partner = mine + bit * (1 - 2 * digit)
            device = (partner, place.space) if axis == "tm" else (place.tm, partner)
            self.partners.append((digit, device))
        half = values.shape[1] // 2
        digit, _ = self.partners[0]
        self.columns = pl.ds(pl.multiple_of(digit * half, lanes), half)
        self.others = pl.ds(pl.multiple_of((1 - digit) * half, lanes), half)
        self.kept = (base, rows)
        self.regions = []
        self.slot = pl.ds(base, rows)
        self.free = base

    def span(self, region):
        start, size = region
        return pl.ds(pl.multiple_of(start, 8), size)

    def move(self, source, target, device):
        self.pending = remote(
            source, target, self.send.at[self.stage], self.receive.at[self.stage], device
        )
        self.pending.start()

    def take(self, size):
        self.slot = pl.ds(self.free, size)
        self.free += size
        return self.inbox.at[self.slot]

    def step(self):
        last = len(self.partners) - 1
        stage = self.stage
        if self.pending is not None:
            self.pending.wait()
            self.pending = None
        if stage == 0:
            rows = self.span(self.kept)
            self.move(self.values.at[rows, self.others], self.landing.at[rows], self.partners[0][1])
        elif stage <= last:
            rows = self.span(self.kept)
            source = self.landing if stage == 1 else self.inbox
            self.values[rows, self.columns] += source[self.slot]
            digit, device = self.partners[stage]
            start, size = self.kept
            if stage < last:
                half = size // 2
                self.regions.append(self.kept)
                self.kept = (start + digit * half, half)
                rows = self.span((start + (1 - digit) * half, half))
                size = half
            self.move(self.values.at[rows, self.columns], self.take(size), device)
        elif stage <= 2 * last:
            rows = self.span(self.kept)
            if stage == last + 1:
                self.whole[rows, self.columns] = self.values[rows, self.columns] + self.inbox[self.slot]
            region = self.whole.at[rows, self.columns]
            self.move(region, region, self.partners[2 * last - stage][1])
            if self.regions:
                self.kept = self.regions.pop()
        self.stage += 1


class KernelSum:
    def __init__(self, place, partial, pieces, rows_tm, whole, send, receive):
        self.place = place
        self.partial, self.pieces, self.rows_tm, self.whole = partial, pieces, rows_tm, whole
        n, m = place.size_space, place.size_tm
        size = pieces.shape[1]
        self.size = size
        mine = place.space

        def part(index):
            return partial.at[pl.ds(pl.multiple_of(index * size, 8), size)]

        self.own = part(mine)
        self.scatter = [
            remote(
                part(lax.rem(mine + d, n)),
                pieces.at[mine],
                send.at[d - 1],
                receive.at[d - 1],
                place.along_space(d),
            )
            for d in range(1, n)
        ]
        slot = rows_tm.at[place.tm]
        self.exchange = [
            remote(slot, slot, send.at[n - 2 + d], receive.at[n - 2 + d], place.along_tm(d))
            for d in range(1, m)
        ]
        slot = whole.at[mine]
        self.gather = [
            remote(slot, slot, send.at[n + m - 3 + d], receive.at[n + m - 3 + d], place.along_space(d))
            for d in range(1, n)
        ]

    def start(self, value):
        rows, total = value.shape[0], self.partial.shape[0]
        self.partial[0:rows] = value
        if total > rows:
            self.partial[rows:total] = jnp.zeros((total - rows, value.shape[1]), f32)
        for copy in self.scatter:
            copy.start()
        self.pieces[pl.ds(self.place.space, 1)] = self.own[...][None]

    def end(self, copies):
        for copy in copies:
            copy.wait_recv()
        for copy in copies:
            copy.wait_send()

    def across(self):
        self.end(self.scatter)
        total = added([self.pieces[i] for i in range(self.place.size_space)])
        self.rows_tm[pl.ds(self.place.tm, 1)] = total[None]
        for copy in self.exchange:
            copy.start()

    def back(self):
        self.end(self.exchange)
        total = added([self.rows_tm[i] for i in range(self.place.size_tm)])
        self.whole[pl.ds(self.place.space, 1)] = total[None]
        for copy in self.gather:
            copy.start()

    def finish(self):
        self.end(self.gather)


def added(parts):
    total = parts[0]
    for part in parts[1:]:
        total = total + part
    return total


def diagonal(shape):
    return lax.broadcasted_iota(jnp.int32, shape, 0) == lax.broadcasted_iota(jnp.int32, shape, 1)


def as_row(column, wide=lanes):
    shape = (column.shape[0], wide)
    return jnp.sum(jnp.where(diagonal(shape), jnp.broadcast_to(column, shape), 0.0), axis=0, keepdims=True)


def as_column(row, chans):
    shape = (chans, row.shape[1])
    return jnp.sum(jnp.where(diagonal(shape), jnp.broadcast_to(row, shape), 0.0), axis=1, keepdims=True)


def per_channel(values):
    return jnp.sum(added(values), axis=1, keepdims=True)


def local_moments(values):
    count = len(values) * values[0].shape[1]
    mean = per_channel(values) / count
    centered = [value - mean for value in values]
    squares = per_channel([value * value for value in centered])
    return jnp.concatenate([as_row(mean), as_row(squares)], axis=0)


def whole_moments(parts, count, chans):
    devices = parts.shape[0]
    means, squares = parts[:, 0:1], parts[:, 1:2]
    middle = jnp.sum(means, axis=0, keepdims=True) / devices
    offset = means - middle
    total = jnp.sum(squares + offset * offset * float(count), axis=0) / float(count * devices)
    return as_column(middle[0], chans), lax.rsqrt(as_column(total, chans) + eps)


def load_taps(kernel, taps, backward):
    chans = kernel.shape[3]
    taps[...] = jnp.zeros(taps.shape, f32)
    for a in range(3):
        for b in range(3):
            for e in range(3):
                tap = kernel[2 - a, 2 - b, 2 - e].T if backward else kernel[a, b, e]
                taps[(e * 3 + a) * 3 + b, :, 0:chans] = tap


def toeplitz(taps, high, low, rows):
    chans = taps.shape[1]
    high[...] = jnp.zeros(high.shape, bf16)
    low[...] = jnp.zeros(low.shape, bf16)
    size = rows * chans
    for e in range(3):
        for a in range(3):
            block = []
            for h in range(rows):
                parts = []
                for b in range(3):
                    tap = taps[(e * 3 + a) * 3 + b]
                    parts.append(pltpu.roll(tap, (h + b) * chans, 1) if h + b else tap)
                block.append(added(parts))
            top, bottom = halves(jnp.concatenate(block, axis=0))
            for t in range(2):
                place = (pl.ds((e * 2 + t) * size, size), pl.ds((t + a) * lanes, lanes))
                high[place] = top
                low[place] = bottom


def side_masks(shape, width):
    place = lax.rem(lax.broadcasted_iota(jnp.int32, shape, 1), width)
    return place > 0, place < width - 1


def later(value, inside):
    return jnp.where(inside, pltpu.roll(value, 1, 1), 0.0)


def earlier(value, inside):
    return jnp.where(inside, pltpu.roll(value, value.shape[1] - 1, 1), 0.0)


def convolve(high, low, grid_high, grid_low, group, rows, chans, width):
    depth = high.shape[1]
    size = 2 * rows * chans
    pairs = (grid_high.shape[0] - 2 * lanes) // (2 * lanes)
    result = []
    for pair in range(pairs):
        span = pl.ds(pair * 2 * lanes, depth)
        value = dot(high[...], grid_high[span, group])
        value = value + dot(high[...], grid_low[span, group])
        value = value + dot(low[...], grid_high[span, group])
        first, last = side_masks((size, value.shape[1]), width)
        result.append(
            later(value[0:size], first)
            + value[size : 2 * size]
            + earlier(value[2 * size : 3 * size], last)
        )
    flat = jnp.concatenate(result, axis=0)
    return [flat[i : i + chans] for i in range(0, flat.shape[0], chans)]


def kernel_gradient(grad, grid_high, grid_low, rows, width):
    chans = grad[0].shape[0]
    total = None
    for pair in range(len(grad) // (2 * rows)):
        block = jnp.concatenate(grad[2 * rows * pair : 2 * rows * (pair + 1)], axis=0)
        first, last = side_masks(block.shape, width)
        taps = jnp.concatenate([earlier(block, last), block, later(block, first)], axis=0)
        high, low = halves(taps)
        span = pl.ds(pair * 2 * lanes, 4 * lanes)
        value = dot_nt(high, grid_high[span])
        value = value + dot_nt(high, grid_low[span])
        value = value + dot_nt(low, grid_high[span])
        total = value if total is None else total + value
    half = rows * chans
    blocks = []
    for e in range(3):
        for a in range(3):
            block = added(
                [
                    total[(e * 2 + t) * half : (e * 2 + t + 1) * half, (t + a) * lanes : (t + a + 1) * lanes]
                    for t in range(2)
                ]
            )
            parts = [block[0:chans]]
            for h in range(1, rows):
                parts.append(pltpu.roll(block[h * chans : (h + 1) * chans], lanes - h * chans, 1))
            blocks.append(added(parts))
    return jnp.concatenate(blocks, axis=0)


def crop_groups(cells, width):
    size = 256 if cells % 256 == 0 and 256 % width == 0 else cells
    return [pl.ds(start, size) for start in range(0, cells, size)]


def joined(parts):
    return [jnp.concatenate(pieces, axis=1) for pieces in zip(*parts)]


class Loads:
    def __init__(self, pairs, semaphores):
        self.copies = [
            pltpu.make_async_copy(source, target, semaphores.at[i])
            for i, (source, target) in enumerate(pairs)
        ]

    def start(self, *which):
        for i in which:
            self.copies[i].start()

    def wait(self, *which):
        for i in which:
            self.copies[i].wait()


def forward_kernel(
    sizes,
    features,
    kernel_one,
    kernel_two,
    gain_one,
    shift_one,
    gain_two,
    shift_two,
    input_high_out,
    input_low_out,
    hidden_high_out,
    hidden_low_out,
    normed_one_out,
    normed_two_out,
    slope_one_out,
    slope_two_out,
    latent_out,
    pooled_out,
    scale_one,
    scale_two,
    peak,
    grid_one,
    grid_two,
    grid_three,
    input_high,
    input_low,
    hidden_high,
    hidden_low,
    normed_one,
    normed_two,
    slope_one,
    slope_two,
    latent,
    pooled,
    taps,
    high,
    low,
    slots_one,
    slots_two,
    halo_send,
    halo_receive,
    share_send,
    share_receive,
    store_done,
):
    width, slab, rows, chans = sizes["width"], sizes["slab"], sizes["rows"], sizes["chans"]
    crops = features.shape[2]
    cells = crops * width
    count = slab * rows * cells
    wide = rows + 2
    everything = pl.ds(0, cells)
    groups = crop_groups(cells, width)
    place = Place(sizes)
    halos = [
        Halo(place, grid, groups, halo_send.at[i], halo_receive.at[i])
        for i, grid in enumerate((grid_one, grid_two, grid_three))
    ]
    shares = [
        Share(place, slots, share_send.at[i], share_receive.at[i])
        for i, slots in enumerate((slots_one, slots_two))
    ]
    stores = Loads(
        [
            (input_high, input_high_out),
            (input_low, input_low_out),
            (hidden_high, hidden_high_out),
            (hidden_low, hidden_low_out),
            (normed_one, normed_one_out),
            (normed_two, normed_two_out),
            (slope_one, slope_one_out),
            (slope_two, slope_two_out),
            (latent, latent_out),
            (pooled, pooled_out),
        ],
        store_done,
    )
    inner, rim = halos[0].inner(), halos[0].rim()
    for halo in halos:
        halo.clear()
    for t in range(slab):
        for h in range(rows):
            for crop in range(crops):
                grid_one[t + 1, h + 1, :, crop * width : (crop + 1) * width] = features[t, h, crop]
    place.barrier()
    halos[0].begin()

    def keep(t, h, group, value, top, bottom):
        span = pl.ds((t * wide + h) * chans, chans)
        top[span, group], bottom[span, group] = halves(value)

    load_taps(kernel_one, taps.at[0], False)
    toeplitz(taps.at[0], high.at[0], low.at[0], rows)
    for t, h in inner:
        keep(t, h, everything, grid_one[t, h], input_high, input_low)
    halos[0].pass_on(0)
    load_taps(kernel_two, taps.at[1], False)
    toeplitz(taps.at[1], high.at[1], low.at[1], rows)
    gains = [as_column(gain[...], chans) for gain in (gain_one, gain_two)]
    shifts = [as_column(shift[...], chans) for shift in (shift_one, shift_two)]
    parts = []
    for number, group in enumerate(groups):
        halos[0].pass_on(number + 1)
        halos[0].finish(number)
        for t, h in rim:
            keep(t, h, group, grid_one[t, h, :, group], input_high, input_low)
        parts.append(convolve(high.at[0], low.at[0], input_high, input_low, group, rows, chans, width))
    halos[0].sent()
    stores.start(0, 1)

    values = joined(parts)
    shares[0].start(local_moments(values))
    for (t, h), value in zip(inner, values):
        grid_two[t, h] = value
    halos[1].begin()
    mean, scale = whole_moments(shares[0].finish(), count, chans)
    scale_one[...] = scale

    def first_layer(t, h, group):
        normed = (grid_two[t, h, :, group] - mean) * scale
        normed_one[t, h, :, group] = normed
        hidden, slope = softplus_parts(gains[0] * normed + shifts[0])
        inside = halos[1].inside(t, h)
        hidden = hidden if inside is None else hidden * inside
        keep(t, h, group, hidden, hidden_high, hidden_low)
        return slope

    for t, h in inner:
        slope_one[t - 1, h - 1] = first_layer(t, h, everything)
    stores.start(6)
    halos[1].pass_on(0)
    parts = []
    for number, group in enumerate(groups):
        halos[1].pass_on(number + 1)
        halos[1].finish(number)
        for t, h in rim:
            first_layer(t, h, group)
        parts.append(convolve(high.at[1], low.at[1], hidden_high, hidden_low, group, rows, chans, width))
    halos[1].sent()
    stores.start(2, 3, 4)

    values = joined(parts)
    shares[1].start(local_moments(values))
    for (t, h), value in zip(inner, values):
        grid_three[t, h] = value
    halos[2].begin()
    mean, scale_again = whole_moments(shares[1].finish(), count, chans)
    scale_two[...] = scale_again

    def second_layer(t, h, group):
        normed = (grid_three[t, h, :, group] - mean) * scale_again
        normed_two[t, h, :, group] = normed
        return gains[1] * normed + shifts[1] + grid_one[t, h, :, group]

    for t, h in inner:
        value, slope = softplus_parts(second_layer(t, h, everything))
        latent[t - 1, h - 1] = value
        slope_two[t - 1, h - 1] = slope
    stores.start(7)
    for t in range(slab // 2):
        pooled[t] = added([latent[2 * t + i, h] for i in range(2) for h in range(rows)])
    stores.start(9)
    halos[2].pass_on(0)
    for number, group in enumerate(groups):
        halos[2].pass_on(number + 1)
        halos[2].finish(number)
        for t, h in rim:
            value = second_layer(t, h, group)
            if t > 0 and h > 0:
                value, _ = softplus_parts(value)
                latent[t - 1, h - 1, :, group] = value * halos[2].inside(t, h)
    halos[2].sent()
    stores.start(5, 8)
    highest = latent[0, 0]
    for t in range(slab + 1):
        for h in range(rows + 1):
            highest = jnp.maximum(highest, latent[t, h])
    peak[...] = jnp.full(peak.shape, jnp.max(highest), f32)
    stores.wait(*range(10))


def query_kernel(
    sizes,
    latent,
    peak,
    cells,
    cotangent,
    weight_one,
    bias_one,
    weight_two,
    bias_two,
    weight_three,
    bias_three,
    weight_four,
    bias_four,
    fields,
    grad_latent,
    grads,
    one,
    one_t,
    two,
    two_t,
    three,
    three_t,
    two_8,
    two_t_8,
    three_8,
    three_t_8,
    four,
    four_t,
    wide_two,
    wide_three,
    wide_four,
    pad_one,
    pad_four,
    along,
    plane,
    inputs,
    cot_pad,
    cot_sum,
    cots,
    grad_biases,
    h1,
    h2,
    h3,
    s1,
    s2,
    s3,
    g1,
    g2,
    g3,
    h1_8,
    h2_8,
    g2_8,
    g3_8,
    scales,
    z_even,
    z_odd,
):
    crop = pl.program_id(0)
    slab, rows, width, chans = sizes["slab"], sizes["rows"], sizes["width"], sizes["chans"]
    hidden = weight_two.shape[0]
    queries = cells.shape[2]
    span_time, span_rows = slab + 1, rows + 1
    weights_at = 4
    tiny = 1e-30
    size_one, size_four = pad_one.shape[0], pad_four.shape[0]

    @pl.when(crop == 0)
    def _():
        known = weight_one.shape[0]
        pad_one[...] = jnp.zeros(pad_one.shape, f32)
        pad_one[0:known] = weight_one[...]
        pad_one[known : known + 1] = bias_one[...]
        pad_four[...] = jnp.zeros(pad_four.shape, f32)
        pad_four[0 : weight_four.shape[0]] = weight_four[...]
        for source, target in ((pad_one, one), (pad_four, four_t)):
            top, bottom = [part.astype(f32) for part in halves(source[...])]
            rest = target.shape[1] - 4 * source.shape[0]
            stack = [top, top, bottom, bottom, jnp.zeros((rest, hidden), f32)]
            target[...] = jnp.concatenate(stack, axis=0).T.astype(bf16)
        for source, target in ((pad_one[0:chans], one_t), (pad_four[...], four)):
            top, bottom = halves(source)
            target[0 : source.shape[0]] = top
            target[source.shape[0] :] = bottom
        for i, weight in enumerate((weight_two, weight_three)):
            scale = 256.0 / jnp.maximum(jnp.max(jnp.abs(weight[...])), tiny)
            scales[weights_at + i] = scale
            pairs = ((two, two_8), (two_t, two_t_8)) if i == 0 else ((three, three_8), (three_t, three_t_8))
            for source, (target, target_8) in zip((weight[...], weight[...].T), pairs):
                top, rest = split(source)
                target[...] = top
                target_8[:, 0:hidden] = (top.astype(f32) * scale).astype(f8)
                target_8[:, hidden:] = (rest * (256.0 * scale)).astype(f8)
        sampled = jnp.sum(jnp.abs(pad_one[0:chans]), axis=0, keepdims=True) * jnp.max(peak[...])
        bound_one = jnp.max(sampled + jnp.sum(jnp.abs(pad_one[chans:]), axis=0, keepdims=True)) + 0.7
        sums = jnp.sum(jnp.abs(weight_two[...]), axis=1, keepdims=True)
        bound_two = jnp.max(sums) * bound_one + jnp.max(jnp.abs(bias_two[...])) + 0.7
        sums = jnp.sum(jnp.abs(pad_four[...]), axis=0, keepdims=True)
        bound_g3 = jnp.max(sums) * jnp.max(jnp.abs(cotangent[...]))
        sums = jnp.sum(jnp.abs(weight_three[...]), axis=0, keepdims=True)
        bound_g2 = jnp.max(sums) * bound_g3
        for i, bound in enumerate((bound_one, bound_two, bound_g2, bound_g3)):
            scales[i] = 256.0 / jnp.maximum(bound, tiny)
        for source, target in ((bias_two, wide_two), (bias_three, wide_three)):
            column = jnp.broadcast_to(source[...], (lanes, hidden)).T
            for start in range(0, chunk, lanes):
                target[:, start : start + lanes] = column
        kind = lax.broadcasted_iota(jnp.int32, wide_four.shape, 0)
        bias = jnp.zeros(wide_four.shape, f32)
        for i in range(weight_four.shape[0]):
            bias = jnp.where(kind == i, bias_four[i], bias)
        wide_four[...] = bias
        inputs[...] = jnp.zeros(inputs.shape, bf16)
        cots[...] = jnp.zeros(cots.shape, bf16)
        for target in (cot_pad, cot_sum, grad_biases, grads):
            target[...] = jnp.zeros(target.shape, f32)

    @pl.when(lax.rem(crop, 2) == 0)
    def _():
        grad_latent[...] = jnp.zeros(grad_latent.shape, f32)

    def product(weights, values, weight_at, value_at, span):
        main, main_8 = weights
        high, parts_8 = values
        cross = dot(main_8[...], parts_8[:, span])
        back = 1.0 / (256.0 * scales[weights_at + weight_at] * scales[value_at])
        return dot(main[...], high[:, span]) + cross * back

    def keep_8(target, span, value, value_at):
        high, parts_8 = target
        top, rest = split(value)
        high[:, span] = top
        scale = scales[value_at]
        parts_8[0:hidden, span] = (rest * (256.0 * scale)).astype(f8)
        parts_8[hidden:, span] = (top.astype(f32) * scale).astype(f8)

    def keep(target, span, value):
        top, bottom = halves(value)
        target[0:hidden, span] = top
        target[hidden:, span] = bottom

    spans = [slice(start, start + chunk) for start in range(0, queries, chunk)]
    latent_parts = jnp.concatenate(halves(latent[...]), axis=1)
    cot_pad[0 : cotangent.shape[1]] = cotangent[pl.ds(crop, 1)][0]
    cot_sum[...] += cot_pad[...]
    offset_time = lax.axis_index("tm") * slab
    offset_rows = lax.axis_index("space") * rows
    offset_width = lax.rem(crop, 2) * width

    for span in spans:
        time = cells[0, pl.ds(crop, 1), span]
        row = cells[1, pl.ds(crop, 1), span]
        place = cells[2, pl.ds(crop, 1), span]
        lane = lax.broadcasted_iota(jnp.int32, (lanes, chunk), 0)
        low = place + offset_width
        weights = jnp.where(lane == low, 1.0 - fraction_width, jnp.where(lane == low + 1, fraction_width, 0.0))
        weights = weights.astype(bf16)
        along[0:lanes, span] = weights
        along[lanes:, span] = weights
        values = dot(latent_parts, along[:, span])
        sampled = None
        for t in range(span_time):
            local = time - offset_time
            weight_time = jnp.where(local == t, 1.0 - fraction_time, jnp.where(local == t - 1, fraction_time, 0.0))
            for h in range(span_rows):
                local = row - offset_rows
                weight_rows = jnp.where(local == h, 1.0 - fraction_rows, jnp.where(local == h - 1, fraction_rows, 0.0))
                weight = weight_time * weight_rows
                index = t * span_rows + h
                plane[index : index + 1, span] = weight
                part = weight * values[index * chans : (index + 1) * chans]
                sampled = part if sampled is None else sampled + part
        coords = [
            2.0 * (time.astype(f32) + fraction_time) / sizes["depth"] - 1.0,
            2.0 * (row.astype(f32) + fraction_rows) / sizes["height"] - 1.0,
            2.0 * (place.astype(f32) + fraction_width) / width - 1.0,
        ]
        kind = lax.broadcasted_iota(jnp.int32, (size_one - chans, chunk), 0)
        extra = jnp.where(kind == 3, 1.0, 0.0)
        for i, coord in enumerate(coords):
            extra = jnp.where(kind == i, coord, extra)
        top, bottom = halves(jnp.concatenate([sampled, extra], axis=0))
        size = top.shape[0]
        for i, part in enumerate((top, bottom, top, bottom)):
            inputs[i * size : (i + 1) * size, span] = part
        top, bottom = halves(cot_pad[:, span])
        size = top.shape[0]
        for i, part in enumerate((top, bottom, top, bottom)):
            cots[i * size : (i + 1) * size, span] = part

    buffers = (z_even, z_odd)
    pending = []
    turn = [0]

    def emit(ahead, after=None):
        buffer = buffers[turn[0] % 2]
        turn[0] += 1
        ahead(buffer)
        flush()
        if after is not None:
            pending.append(lambda: after(buffer))

    def flush():
        while pending:
            pending.pop()()

    def forward(kept, slope_kept, span, bias, value_at=None):
        def after(buffer):
            value = buffer[...] if bias is None else buffer[...] + bias[...]
            value, slope = softplus_parts(value)
            if value_at is None:
                keep(kept, span, value)
            else:
                keep_8(kept, span, value, value_at)
            slope_kept[:, span] = slope

        return after

    def backward(kept, slope_kept, span, bias, value_at=None):
        def after(buffer):
            grad = buffer[...] * slope_kept[:, span]
            if value_at is None:
                keep(kept, span, grad)
            else:
                keep_8(kept, span, grad, value_at)
            if bias is not None:
                grad_biases[bias] += added([grad[:, i : i + lanes] for i in range(0, chunk, lanes)])

        return after

    def store(make):
        def ahead(buffer):
            buffer[...] = make()

        return ahead

    def outer_part(start, grads_here, values, grads_at, values_at, part):
        def ahead(buffer):
            here = slice(part * chunk, (part + 1) * chunk)
            low = slice(hidden + part * chunk, hidden + (part + 1) * chunk)
            cross = dot_nt(grads_here[1][0:hidden], values[1][low])
            cross = cross + dot_nt(grads_here[1][hidden:], values[1][here])
            back = 1.0 / (256.0 * scales[grads_at] * scales[values_at])
            grads[start : start + hidden, here] += dot_nt(grads_here[0][...], values[0][here]) + cross * back

        return ahead

    def fields_part(span):
        def ahead(buffer):
            both = dot(four[...], h3[0:hidden, span])
            value = both[0:size_four] + both[size_four:] + dot(four[0:size_four], h3[hidden:, span])
            fields[0, :, span] = (value + wide_four[...])[0 : fields.shape[1]]

        return ahead

    def grad_four_part(buffer):
        both = dot_nt(cots[0 : 2 * size_four], h3[0:hidden])
        total = both[0:size_four] + both[size_four:]
        total = total + dot_nt(cots[0:size_four], h3[hidden:])
        start = 2 * hidden + size_one
        grads[start : start + size_four] += total

    def grad_one_part(buffer):
        both = dot_nt(inputs[0 : 2 * size_one], g1[0:hidden])
        total = both[0:size_one] + both[size_one:]
        total = total + dot_nt(inputs[0:size_one], g1[hidden:])
        grads[2 * hidden : 2 * hidden + size_one] += total

    def latent_part(span):
        def ahead(buffer):
            both = dot(one_t[...], g1[0:hidden, span])
            buffer[0:chans] = both[0:chans] + both[chans:] + dot(one_t[0:chans], g1[hidden:, span])

        def after(buffer):
            grad = buffer[0:chans]
            spread = [plane[i : i + 1, span] * grad for i in range(span_time * span_rows)]
            top, bottom = halves(jnp.concatenate(spread, axis=0))
            both = dot_nt(jnp.concatenate([top, bottom], axis=0), along[0:lanes, span])
            grad_latent[...] += both[0 : top.shape[0]] + both[top.shape[0] :]

        return ahead, after

    parts = hidden // chunk
    first, second = (h1, h1_8), (h2, h2_8)
    third_grad, second_grad = (g3, g3_8), (g2, g2_8)
    for span in spans:
        emit(store(lambda: dot(one[...], inputs[:, span])), forward(first, s1, span, None, 0))
    for span in spans:
        emit(store(lambda: product((two, two_8), first, 0, 0, span)), forward(second, s2, span, wide_two, 1))
    for span in spans:
        emit(store(lambda: product((three, three_8), second, 1, 1, span)), forward(h3, s3, span, wide_three))
    for span in spans:
        emit(store(lambda: dot(four_t[...], cots[:, span])), backward(third_grad, s3, span, 1, 3))
        emit(fields_part(span))
    emit(grad_four_part)
    for span in spans:
        emit(
            store(lambda: product((three_t, three_t_8), third_grad, 1, 3, span)),
            backward(second_grad, s2, span, 0, 2),
        )
    for part in range(parts):
        emit(outer_part(hidden, third_grad, second, 3, 1, part))
    for span in spans:
        emit(store(lambda: product((two_t, two_t_8), second_grad, 0, 2, span)), backward(g1, s1, span, None))
    outers = [outer_part(0, second_grad, first, 2, 0, part) for part in range(parts)]
    for i, span in enumerate(spans):
        emit(*latent_part(span))
        if i % 2 and outers:
            emit(outers.pop(0))
    for rest in outers:
        emit(rest)
    emit(grad_one_part)
    flush()

    @pl.when(crop == pl.num_programs(0) - 1)
    def _():
        start = 2 * hidden + size_one + size_four
        for i in range(2):
            grads[start + i : start + i + 1] = jnp.sum(grad_biases[i].T, axis=0, keepdims=True)
        total = jnp.sum(cot_sum[...], axis=1, keepdims=True)
        grads[start + 2 : start + 3] = as_row(total, hidden)


def backward_kernel(
    sizes,
    grad_latent_in,
    upsampled_in,
    input_high_in,
    input_low_in,
    hidden_high_in,
    hidden_low_in,
    normed_one_in,
    normed_two_in,
    slope_one_in,
    slope_two_in,
    grads_in,
    scale_one,
    scale_two,
    gain_one,
    gain_two,
    kernel_one,
    kernel_two,
    grad_features,
    grads_out,
    grad_kernels,
    sums,
    folded,
    upsampled,
    input_high,
    input_low,
    hidden_high,
    hidden_low,
    normed_one,
    normed_two,
    slope_one,
    slope_two,
    grads,
    landing,
    inbox,
    whole,
    arrived_time,
    arrived_rows,
    grid_one,
    grid_two,
    grid_high,
    grid_low,
    grad_summed,
    taps,
    high,
    low,
    partial,
    pieces,
    rows_tm,
    gathered,
    slots_one,
    slots_two,
    halo_send,
    halo_receive,
    share_send,
    share_receive,
    sum_send,
    sum_receive,
    reduce_send,
    reduce_receive,
    load_done,
):
    width, slab, rows, chans = sizes["width"], sizes["slab"], sizes["rows"], sizes["chans"]
    wide = rows + 2
    cells = upsampled.shape[2]
    crops = cells // width
    place = Place(sizes)
    count = float(slab * rows * cells * place.devices)
    everything = pl.ds(0, cells)
    groups = crop_groups(cells, width)
    halo_one = Halo(place, grid_one, groups, halo_send.at[0], halo_receive.at[0])
    halo_two = Halo(place, grid_two, groups, halo_send.at[1], halo_receive.at[1])
    share_one = Share(place, slots_one, share_send.at[0], share_receive.at[0])
    share_two = Share(place, slots_two, share_send.at[1], share_receive.at[1])
    kernel_sums = [
        KernelSum(
            place,
            partial.at[i],
            pieces.at[i],
            rows_tm.at[i],
            gathered.at[i],
            sum_send.at[i],
            sum_receive.at[i],
        )
        for i in range(2)
    ]
    bits_tm = [("tm", 1 << i) for i in range(place.size_tm.bit_length() - 1)]
    bits_space = [("space", 1 << i) for i in range(place.size_space.bit_length() - 1)]
    orders = [
        [bits_space[0]] + bits_tm[1:] + bits_space[1:] + bits_tm[:1],
        bits_space + bits_tm[1:] + bits_tm[:1],
    ]
    half = grads.shape[0] // 2
    reductions = [
        Reduction(
            place,
            grads,
            landing,
            inbox,
            whole,
            i * half,
            half,
            orders[i],
            reduce_send.at[i],
            reduce_receive.at[i],
        )
        for i in range(2)
    ]
    total_steps = 2 * len(orders[0])

    def reduce_step(*which):
        for i in which:
            if reductions[i].stage < total_steps:
                reductions[i].step()

    loads = Loads(
        [
            (grad_latent_in, folded),
            (grads_in, grads),
            (upsampled_in, upsampled),
            (slope_two_in, slope_two),
            (normed_two_in, normed_two),
            (hidden_high_in, hidden_high),
            (hidden_low_in, hidden_low),
            (slope_one_in, slope_one),
            (normed_one_in, normed_one),
            (input_high_in, input_high),
            (input_low_in, input_low),
        ],
        load_done,
    )
    loads.start(*range(11))
    halo_one.clear()
    halo_two.clear()
    up_t, up_h = place.along_tm(1), place.along_space(1)
    low_t, high_t = place.tm > 0, place.tm < place.size_tm - 1
    low_h, high_h = place.space > 0, place.space < place.size_space - 1

    @pl.when(jnp.logical_not(low_t))
    def _():
        arrived_time[...] = jnp.zeros(arrived_time.shape, f32)

    @pl.when(jnp.logical_not(low_h))
    def _():
        arrived_rows[...] = jnp.zeros(arrived_rows.shape, f32)

    send, receive = halo_send.at[2, 0], halo_receive.at[2, 0]
    time_copy = remote(folded.at[pl.ds(slab, 1)], arrived_time, send.at[0], receive.at[0], up_t)
    rows_copy = remote(
        folded.at[pl.ds(1, slab - 1), pl.ds(rows, 1)],
        arrived_rows.at[pl.ds(1, slab - 1)],
        send.at[1],
        receive.at[1],
        up_h,
    )
    corner_copy = remote(
        folded.at[pl.ds(0, 1), pl.ds(rows, 1)],
        arrived_rows.at[pl.ds(0, 1)],
        send.at[2],
        receive.at[2],
        up_h,
    )
    loads.wait(0)
    place.barrier()

    @pl.when(high_t)
    def _():
        time_copy.start()

    @pl.when(high_h)
    def _():
        rows_copy.start()

    loads.wait(1)
    reduce_step(0, 1)
    load_taps(kernel_two, taps.at[1], True)
    toeplitz(taps.at[1], high.at[1], low.at[1], rows)
    load_taps(kernel_one, taps.at[0], True)
    toeplitz(taps.at[0], high.at[0], low.at[0], rows)
    gains = [as_column(gain[...], chans) for gain in (gain_one, gain_two)]

    @pl.when(low_t)
    def _():
        time_copy.wait_recv()

    folded[0:1] += arrived_time[...]

    @pl.when(high_h)
    def _():
        corner_copy.start()

    reduce_step(0, 1)

    @pl.when(low_h)
    def _():
        rows_copy.wait_recv()
        corner_copy.wait_recv()

    @pl.when(high_t)
    def _():
        time_copy.wait_send()

    @pl.when(high_h)
    def _():
        rows_copy.wait_send()
        corner_copy.wait_send()

    folded[0:slab, 0:1] += arrived_rows[...]
    loads.wait(2, 3, 4)
    reduce_step(0, 1)
    inner, rim = halo_one.inner(), halo_one.rim()

    def norm_sums(grads_here, normed):
        cross = [grad * normed[t, h] for (t, h), grad in zip(inner, grads_here)]
        return jnp.concatenate(
            [as_row(per_channel(grads_here)), as_row(per_channel(cross))], axis=0
        )

    def norm_terms(parts, scale, gain):
        result = jnp.sum(parts, axis=0)
        total = as_column(result[0:1], chans) / count
        cross = as_column(result[1:2], chans) / count
        return result, total, cross, gain * scale[...]

    def keep(t, h, group, value):
        span = pl.ds((t * wide + h) * chans, chans)
        grid_high[span, group], grid_low[span, group] = halves(value)

    def norm_grads(halo, normed, terms, taps_at, before):
        _, total, cross, factor = terms
        grid = halo.grid

        def through(t, h, group):
            return factor * (grid[t, h, :, group] - total - normed[t, h, :, group] * cross)

        values = []
        for t, h in inner:
            value = through(t, h, everything)
            values.append(value)
            keep(t, h, everything, value)
        halo.pass_on(0)
        before(values)
        parts = []
        for number, group in enumerate(groups):
            halo.pass_on(number + 1)
            halo.finish(number)
            for t, h in rim:
                keep(t, h, group, through(t, h, group) * halo.inside(t, h))
            parts.append(
                convolve(high.at[taps_at], low.at[taps_at], grid_high, grid_low, group, rows, chans, width)
            )
        halo.sent()
        return joined(parts)

    values = []
    for t, h in inner:
        value = folded[t - 1, h - 1] + upsampled[(t - 1) // 2]
        value = value * slope_two[t - 1, h - 1]
        grad_summed[t - 1, h - 1] = value
        grid_two[t, h] = value
        values.append(value)
    share_two.start(norm_sums(values, normed_two))
    halo_two.begin()
    terms = norm_terms(share_two.finish(), scale_two, gains[1])
    sums[1] = terms[0]
    reduce_step(0, 1)

    def before(values):
        loads.wait(5, 6)
        kernel_sums[1].start(kernel_gradient(values, hidden_high, hidden_low, rows, width))
        reduce_step(0, 1)

    values = norm_grads(halo_two, normed_two, terms, 1, before)
    loads.wait(7, 8)
    values = [value * slope_one[t - 1, h - 1] for (t, h), value in zip(inner, values)]
    share_one.start(norm_sums(values, normed_one))
    for (t, h), value in zip(inner, values):
        grid_one[t, h] = value
    halo_one.begin()
    kernel_sums[1].across()
    reduce_step(0, 1)
    terms = norm_terms(share_one.finish(), scale_one, gains[0])
    sums[0] = terms[0]
    reduce_step(0, 1)

    def before(values):
        kernel_sums[1].back()
        loads.wait(9, 10)
        kernel_sums[0].start(kernel_gradient(values, input_high, input_low, rows, width))
        reduce_step(0, 1)

    values = norm_grads(halo_one, normed_one, terms, 0, before)
    kernel_sums[0].across()
    reduce_step(0, 1)
    for (t, h), value in zip(inner, values):
        value = value + grad_summed[t - 1, h - 1]
        for crop in range(crops):
            grad_features[t - 1, h - 1, crop] = value[:, crop * width : (crop + 1) * width]
    kernel_sums[0].back()
    for i in range(2):
        while reductions[i].stage < total_steps:
            reduce_step(i)
    grads_out[...] = whole[...]
    for i in range(2):
        kernel_sums[i].finish()
        size = grad_kernels.shape[1]
        grad_kernels[i] = gathered[i].reshape(-1, lanes)[0:size]


def closing_kernel(
    sizes,
    grads,
    grad_kernels,
    sums,
    kernel_one,
    gain_one,
    shift_one,
    kernel_two,
    gain_two,
    shift_two,
    one,
    bias_one,
    two,
    bias_two,
    three,
    bias_three,
    four,
    bias_four,
):
    chans = sizes["chans"]
    hidden = two.shape[0]
    for i, kernel in enumerate((kernel_one, kernel_two)):
        for e in range(3):
            for a in range(3):
                block = grad_kernels[i, (e * 3 + a) * chans : (e * 3 + a + 1) * chans]
                for b in range(3):
                    kernel[a, b, e] = block[:, b * chans : (b + 1) * chans]
    for i, (gain, shift) in enumerate(((gain_one, shift_one), (gain_two, shift_two))):
        shift[...] = sums[i, 0:1, 0:chans]
        gain[...] = sums[i, 1:2, 0:chans]
    two[...] = grads[0:hidden]
    three[...] = grads[hidden : 2 * hidden]
    start = 2 * hidden
    known = one.shape[0]
    one[...] = grads[start : start + known]
    bias_one[...] = grads[start + known : start + known + 1]
    start += sizes["rows_one"]
    four[...] = grads[start : start + four.shape[0]]
    start += sizes["rows_four"]
    bias_two[...] = grads[start : start + 1]
    bias_three[...] = grads[start + 1 : start + 2]
    bias_four[...] = grads[start + 2 : start + 3, 0 : bias_four.shape[1]]


def in_vmem(count):
    return [pl.BlockSpec(memory_space=VMEM)] * count


def anywhere(count):
    return [pl.BlockSpec(memory_space=pl.ANY)] * count


def struct(shape, dtype=f32):
    return jax.ShapeDtypeStruct(shape, dtype)


def scratch(structs):
    return [VMEM(item.shape, item.dtype) for item in structs]


def per_device(
    mesh_sizes,
    features,
    conv_first,
    gain_first,
    shift_first,
    conv_second,
    gain_second,
    shift_second,
    weight_one,
    bias_one,
    weight_two,
    bias_two,
    weight_three,
    bias_three,
    weight_four,
    bias_four,
    query_cells,
    field_cotangent,
    pooled_cotangent,
):
    crops, chans, slab, rows, width = features.shape
    queries = query_cells.shape[2]
    hidden, known = weight_one.shape
    field_count = weight_four.shape[0]
    size_tm, size_space = mesh_sizes
    devices = size_tm * size_space
    cells = crops * width
    rows_one = -(-(known + 1) // 16) * 16
    rows_four = 16
    sizes = {
        "tm": size_tm,
        "space": size_space,
        "slab": slab,
        "rows": rows,
        "width": width,
        "chans": chans,
        "depth": slab * size_tm,
        "height": rows * size_space,
        "rows_one": rows_one,
        "rows_four": rows_four,
    }
    span, wide = slab + 2, rows + 2
    matrix = (2, 6 * rows * chans, 4 * wide * chans)
    taps = VMEM((2, 27, chans, lanes), f32)
    memory = pltpu.CompilerParams(vmem_limit_bytes=56 * 2**20)

    grid = jnp.transpose(features, (2, 3, 0, 1, 4))
    kernels = [jnp.transpose(kernel, (2, 3, 4, 0, 1)) for kernel in (conv_first, conv_second)]
    gains = [gain_first[None], gain_second[None]]
    shifts = [shift_first[None], shift_second[None]]
    block = struct((slab, rows, chans, cells))
    padded = struct((span, wide, chans, cells))
    flat = struct((span * wide * chans, cells), bf16)
    column = struct((chans, 1))
    slots = VMEM((devices, 2, lanes), f32)
    kept = [flat] * 4 + [padded] * 2 + [block] * 2
    kept += [struct((slab + 1, rows + 1, chans, cells)), struct((slab // 2, chans, cells))]
    copies = pltpu.SemaphoreType.DMA
    group_count = len(crop_groups(cells, width))
    (
        input_high,
        input_low,
        hidden_high,
        hidden_low,
        normed_one,
        normed_two,
        slope_one,
        slope_two,
        latent,
        pool_part,
        scale_one,
        scale_two,
        peak,
    ) = pl.pallas_call(
        functools.partial(forward_kernel, sizes),
        out_shape=kept + [column] * 2 + [struct((8, lanes))],
        in_specs=in_vmem(7),
        out_specs=anywhere(10) + in_vmem(3),
        scratch_shapes=[
            *scratch([padded] * 3 + kept),
            taps,
            VMEM(matrix, bf16),
            VMEM(matrix, bf16),
            slots,
            slots,
            copies((3, group_count, 8)),
            copies((3, group_count, 8)),
            copies((2, devices - 1)),
            copies((2, devices - 1)),
            copies((10,)),
        ],
        compiler_params=pltpu.CompilerParams(
            collective_id=0, has_side_effects=True, vmem_limit_bytes=56 * 2**20
        ),
        name="forward_block",
    )(grid, *kernels, gains[0], shifts[0], gains[1], shifts[1])
    pooled = pool_part.reshape(slab // 2, chans, crops, width // 2, 2).sum(axis=4) * (0.25 / rows)
    pooled = jnp.transpose(pooled, (2, 1, 0, 3))[:, :, :, None, :]

    sample_rows = (slab + 1) * (rows + 1)
    unit = 8 << (devices.bit_length() - 3)
    reduce_rows = -(-(2 * hidden + rows_one + rows_four + 8) // (2 * unit)) * 2 * unit
    pair_block = pl.BlockSpec((sample_rows * chans, lanes), lambda n: (0, n // 2))
    crop_block = pl.BlockSpec((1, field_count, queries), lambda n: (n, 0, 0))

    def constant(shape):
        return pl.BlockSpec(shape, lambda n: (0,) * len(shape))

    operands = [
        latent.reshape(sample_rows * chans, cells),
        peak,
        query_cells,
        jnp.transpose(field_cotangent, (1, 0, 2)),
        jnp.transpose(weight_one),
        bias_one[None],
        weight_two,
        bias_two[None],
        weight_three,
        bias_three[None],
        weight_four,
        bias_four,
    ]
    specs = [pair_block]
    specs += [constant(operand.shape) for operand in operands[1:-1]]
    specs += [pl.BlockSpec(memory_space=pltpu.SMEM)]
    outs = [
        struct((crops, field_count, queries)),
        struct((sample_rows * chans, cells)),
        struct((reduce_rows, hidden)),
    ]
    fields, grad_latent, grads = pl.pallas_call(
        functools.partial(query_kernel, sizes),
        grid=(crops,),
        out_shape=outs,
        in_specs=specs,
        out_specs=[crop_block, pair_block, constant(outs[2].shape)],
        scratch_shapes=[
            VMEM((hidden, 256), bf16),
            VMEM((2 * chans, hidden), bf16),
            *[VMEM((hidden, hidden), bf16)] * 4,
            *[VMEM((hidden, 2 * hidden), f8)] * 4,
            VMEM((2 * rows_four, hidden), bf16),
            VMEM((hidden, lanes), bf16),
            VMEM((hidden, chunk), f32),
            VMEM((hidden, chunk), f32),
            VMEM((rows_four, chunk), f32),
            VMEM((rows_one, hidden), f32),
            VMEM((rows_four, hidden), f32),
            VMEM((2 * lanes, queries), bf16),
            VMEM((-(-sample_rows // 8) * 8, queries), f32),
            VMEM((256, queries), bf16),
            VMEM((rows_four, queries), f32),
            VMEM((rows_four, queries), f32),
            VMEM((lanes, queries), bf16),
            VMEM((2, hidden, lanes), f32),
            *[VMEM((hidden, queries), bf16)] * 2,
            VMEM((2 * hidden, queries), bf16),
            *[VMEM((hidden, queries), f32)] * 3,
            VMEM((2 * hidden, queries), bf16),
            *[VMEM((hidden, queries), bf16)] * 2,
            *[VMEM((2 * hidden, queries), f8)] * 4,
            pltpu.SMEM((8,), f32),
            *[VMEM((hidden, chunk), f32)] * 2,
        ],
        compiler_params=pltpu.CompilerParams(
            dimension_semantics=("arbitrary",), vmem_limit_bytes=56 * 2**20
        ),
        name="query_network",
    )(*operands)

    upsampled = jnp.transpose(pooled_cotangent[:, :, :, 0], (2, 1, 0, 3)) * (0.25 / rows)
    upsampled = jnp.broadcast_to(upsampled[..., None], upsampled.shape + (2,))
    upsampled = upsampled.reshape(slab // 2, chans, cells)
    kernel_rows = 9 * chans
    piece = -(-kernel_rows // (8 * size_space)) * 8
    sum_copies = 2 * size_space + size_tm - 3
    reduce_block = struct((reduce_rows, hidden))
    half_block = struct((reduce_rows, hidden // 2))
    loaded = [struct((slab + 1, rows + 1, chans, cells)), struct((slab // 2, chans, cells))]
    loaded += [flat] * 4 + [padded] * 2 + [block] * 2 + [reduce_block]
    grad_features, grads, grad_kernels, sums = pl.pallas_call(
        functools.partial(backward_kernel, sizes),
        out_shape=[
            struct((slab, rows, crops, chans, width)),
            reduce_block,
            struct((2, kernel_rows, lanes)),
            struct((2, 2, lanes)),
        ],
        in_specs=anywhere(11) + in_vmem(6),
        out_specs=in_vmem(4),
        scratch_shapes=[
            *scratch(loaded),
            *scratch([half_block] * 2 + [reduce_block]),
            VMEM((1, rows + 1, chans, cells), f32),
            VMEM((slab, 1, chans, cells), f32),
            *scratch([padded] * 2 + [flat] * 2 + [block]),
            taps,
            VMEM(matrix, bf16),
            VMEM(matrix, bf16),
            VMEM((2, size_space * piece, lanes), f32),
            VMEM((2, size_space, piece, lanes), f32),
            VMEM((2, size_tm, piece, lanes), f32),
            VMEM((2, size_space, piece, lanes), f32),
            slots,
            slots,
            copies((3, group_count, 8)),
            copies((3, group_count, 8)),
            copies((2, devices - 1)),
            copies((2, devices - 1)),
            copies((2, sum_copies)),
            copies((2, sum_copies)),
            copies((2, 2 * devices.bit_length())),
            copies((2, 2 * devices.bit_length())),
            copies((11,)),
        ],
        compiler_params=pltpu.CompilerParams(
            collective_id=1, has_side_effects=True, vmem_limit_bytes=56 * 2**20
        ),
        name="backward_block",
    )(
        grad_latent.reshape(slab + 1, rows + 1, chans, cells),
        upsampled,
        input_high,
        input_low,
        hidden_high,
        hidden_low,
        normed_one,
        normed_two,
        slope_one,
        slope_two,
        grads,
        scale_one,
        scale_two,
        gains[0],
        gains[1],
        *kernels,
    )
    row = struct((1, chans))
    wide_row = struct((1, hidden))
    taps_shape = struct((3, 3, 3, chans, chans))
    closing = pl.pallas_call(
        functools.partial(closing_kernel, sizes),
        out_shape=[
            taps_shape,
            row,
            row,
            taps_shape,
            row,
            row,
            struct((known, hidden)),
            wide_row,
            struct((hidden, hidden)),
            wide_row,
            struct((hidden, hidden)),
            wide_row,
            struct((field_count, hidden)),
            struct((1, field_count)),
        ],
        in_specs=in_vmem(3),
        out_specs=in_vmem(14),
        compiler_params=memory,
        name="closing",
    )(grads, grad_kernels, sums)
    closing = list(closing)
    for i in (0, 3):
        closing[i] = jnp.transpose(closing[i], (3, 4, 0, 1, 2))
    closing[6] = jnp.transpose(closing[6])
    for i in (1, 2, 4, 5, 7, 9, 11, 13):
        closing[i] = closing[i][0]
    return (
        jnp.transpose(fields, (1, 0, 2)),
        pooled,
        jnp.transpose(grad_features, (2, 3, 0, 1, 4)),
        *closing,
    )


def solution(mesh):
    placed = (P(None, None, "tm", "space", None),) + (P(),) * 14
    placed += (P(None, None, ("tm", "space")),) * 2 + (P(None, None, "tm", "space", None),)
    return jax.shard_map(
        functools.partial(per_device, (mesh.shape["tm"], mesh.shape["space"])),
        mesh=mesh,
        in_specs=placed,
        out_specs=(
            P(None, None, ("tm", "space")),
            P(None, None, "tm", "space", None),
            P(None, None, "tm", "space", None),
        )
        + (P(),) * 14,
        check_vma=False,
    )
```
